256 devices in a mesh: rows: 32 (over z, x), rep: 8 (over y, core).
Axes of the slice: x: 4, y: 4, z: 8, core: 2. Of those that a mesh axis runs over, the one named last changes fastest.
Arguments:
- features: bfloat16 [65536, 128], P(('rows', 'rep')), may hold values from -6 to 6
- weights: bfloat16 [128, 256], replicated, may hold values from -0.5 to 0.5
- bias_vector: float32 [256], replicated, may hold values from -3 to 3
- block_values: bfloat16 [32, 8, 320, 128, 128], P('rows', 'rep'), may hold values from -0.0390625 to 0.0390625
- block_rows: int32 [32, 8, 320], P('rows', 'rep'), may hold values from 0 to 15
- block_cols: int32 [32, 8, 320], P('rows', 'rep'), may hold values from 0 to 63
- block_live: int32 [32, 8], P('rows', 'rep'), may hold values from 80 to 320, as said below
- cotangent: bfloat16 [65536, 256], P(('rows', 'rep')), may hold values from -6 to 6
Outputs:
- hidden: bfloat16 [65536, 256], P(('rows', 'rep'))
- grad_features: float32 [65536, 128], P(('rows', 'rep'))
- grad_weights: float32 [128, 256], replicated
- grad_bias: float32 [256], replicated
The draws below stay inside these ranges and needn't reach their ends.
Inputs may be any that keep to these rules, and one draw needn't show every extreme that they name: `block_live`: every slot past the live count is unused; some index of the mesh uses all 320 slots.
All inputs are finite; a program needn't handle non-finite values.
Results may differ from the reference program's by a relative error of at most 0.007.
Values may be sent and summed in bfloat16 or wider, within the bound.
A program may use at most 128 MiB of HBM per device.

```python
import jax
import jax.numpy as jnp
from jax import lax

F = 128
HID = 256
BS = 128
SLAB_BLK = 16
BLK_DEV = 320
SH = 256
COLBLK = 64
NODES = 65536
N_ROWS = 32
N_REP = 8


def draw_block_live(key, part):
    key = jax.random.fold_in(key, 11)
    first_key, second_key, third_key = jax.random.split(key, 3)
    devices_all = N_ROWS * N_REP
    base_count = jax.random.randint(first_key, (devices_all,), BLK_DEV // 4, BLK_DEV // 2 + 1)
    filled = jax.random.randint(second_key, (devices_all,), 0, 8) == 0
    chosen = jax.random.randint(third_key, (), 0, devices_all)
    filled = filled | (jnp.arange(devices_all) == chosen)
    return jnp.where(filled, BLK_DEV, base_count).reshape(N_ROWS, N_REP).astype(jnp.int32)


def set_ends(entries, stream_key, smallest, largest):
    shape = entries.shape
    spot = [jax.random.randint(jax.random.fold_in(stream_key, axis), (), 0, shape[axis]) for axis in range(len(shape))]
    entries = entries.at[tuple(spot)].set(smallest)
    longest = shape.index(max(shape))
    spot[longest] = (spot[longest] + 1) % shape[longest]
    return entries.at[tuple(spot)].set(largest)


def levels(own_key, shape, cuts, smallest, largest):
    def one(position, blocks):
        draws = jax.random.uniform(jax.random.fold_in(jax.random.fold_in(own_key, 6), position), (blocks,), jnp.float32, smallest / len(cuts), largest / len(cuts))
        return jnp.repeat(jnp.exp(draws), shape[position] // blocks).reshape((-1,) + (1,) * (len(shape) - position - 1))

    factor_of = one(*cuts[0])
    for cut in cuts[1:]:
        factor_of = factor_of * one(*cut)
    return factor_of


def noise(stream_key, shape, deviation, limit, cuts=(), dtype=jnp.bfloat16):
    entries = deviation * jax.random.normal(stream_key, shape, jnp.float32)
    if cuts:
        entries = entries * levels(stream_key, shape, cuts, -0.22, 0.18)
    return jnp.clip(entries, -limit, limit).astype(dtype)


def setup_inputs(seed: int = 0) -> dict:
    seeds = jax.random.split(jax.random.key(seed), 9)
    features = noise(seeds[0], (NODES, F), 1.0, 6.0, ((0, 256),))
    weights = noise(seeds[1], (F, HID), F ** -0.5, 0.5)
    bias_vector = noise(seeds[2], (HID,), 0.5, 3.0, (), jnp.float32)
    block_values = noise(seeds[3], (N_ROWS, N_REP, BLK_DEV, BS, BS), (BS * BLK_DEV * N_REP // SLAB_BLK) ** -0.5, 0.0390625, ((0, 32), (1, 8)))
    block_rows = set_ends(jax.random.randint(seeds[4], (N_ROWS, N_REP, BLK_DEV), 0, SLAB_BLK), jax.random.fold_in(seeds[4], 1), 0, SLAB_BLK - 1).astype(jnp.int32)
    block_cols = set_ends(jax.random.randint(seeds[5], (N_ROWS, N_REP, BLK_DEV), 0, COLBLK), jax.random.fold_in(seeds[5], 1), 0, COLBLK - 1).astype(jnp.int32)
    block_live = draw_block_live(jax.random.fold_in(seeds[8], 71), 0)
    cotangent = noise(seeds[7], (NODES, HID), 1.0, 6.0, ((0, 256),))
    return dict(features=features, weights=weights, bias_vector=bias_vector, block_values=block_values, block_rows=block_rows, block_cols=block_cols, block_live=block_live, cotangent=cotangent)


HIGHEST = lax.Precision.HIGHEST

def forward_terms(values, row_index, col_index, live_count, panel):
    picked = panel[col_index]
    products = jnp.einsum('bpq,bqf->bpf', values.astype(jnp.float32), picked.astype(jnp.float32), precision=HIGHEST)
    slot_weight = (jnp.arange(BLK_DEV) < live_count).astype(jnp.float32)
    one_hot = (row_index[None, :] == jnp.arange(SLAB_BLK)[:, None]).astype(jnp.float32) * slot_weight[None, :]
    return jnp.einsum('ib,bpf->ipf', one_hot, products, precision=HIGHEST)

def backward_terms(values, row_index, col_index, live_count, slab):
    picked = slab[row_index]
    products = jnp.einsum('bpq,bpf->bqf', values.astype(jnp.float32), picked.astype(jnp.float32), precision=HIGHEST)
    slot_weight = (jnp.arange(BLK_DEV) < live_count).astype(jnp.float32)
    one_hot = (col_index[None, :] == jnp.arange(COLBLK)[:, None]).astype(jnp.float32) * slot_weight[None, :]
    return jnp.einsum('kb,bqf->kqf', one_hot, products, precision=HIGHEST)

def reference(features, weights, bias_vector, block_values, block_rows, block_cols, block_live, cotangent):
    pieces = features.reshape(N_ROWS, N_REP, SH, F)
    panels = jnp.transpose(pieces, (1, 0, 2, 3)).reshape(N_REP, COLBLK, BS, F)

    def slab_total(row_group):

        def device_term(rep_index):
            return forward_terms(block_values[row_group, rep_index], block_rows[row_group, rep_index], block_cols[row_group, rep_index], block_live[row_group, rep_index], panels[rep_index])
        return lax.optimization_barrier(jnp.sum(lax.map(device_term, jnp.arange(N_REP)), axis=0))
    partial_value = lax.map(slab_total, jnp.arange(N_ROWS))
    aggregate = partial_value.reshape(NODES, F).astype(jnp.bfloat16)
    preact = jnp.dot(aggregate, weights, preferred_element_type=jnp.float32) + bias_vector
    hidden = jax.nn.silu(preact).astype(jnp.bfloat16)
    sigma = jax.nn.sigmoid(preact)
    deriv = sigma * (1.0 + preact * (1.0 - sigma))
    grad_pre = (cotangent.astype(jnp.float32) * deriv).astype(jnp.bfloat16)
    scale = 1.0 / jnp.sqrt(jnp.float32(NODES))
    grad_weights = jnp.dot(aggregate.T, grad_pre, preferred_element_type=jnp.float32) * scale
    grad_bias = lax.optimization_barrier(jnp.sum(grad_pre.astype(jnp.float32), axis=0)) * scale
    grad_agg = jnp.dot(grad_pre, weights.T, preferred_element_type=jnp.float32).astype(jnp.bfloat16)
    slabs = grad_agg.reshape(N_ROWS, SLAB_BLK, BS, F)

    def column_total(rep_index):

        def device_term(row_group):
            return backward_terms(block_values[row_group, rep_index], block_rows[row_group, rep_index], block_cols[row_group, rep_index], block_live[row_group, rep_index], slabs[row_group])
        return lax.optimization_barrier(jnp.sum(lax.map(device_term, jnp.arange(N_ROWS)), axis=0))
    columns = lax.map(column_total, jnp.arange(N_REP))
    grad_features = jnp.transpose(columns.reshape(N_REP, N_ROWS, SH, F), (1, 0, 2, 3)).reshape(NODES, F)
    return (hidden, grad_features, grad_weights, grad_bias)
```

```python
import functools
import math

import jax
import jax.numpy as jnp
from jax import lax
from jax.experimental import pallas as pl
from jax.experimental.pallas import tpu as pltpu
from jax.sharding import PartitionSpec as P

MESH = pl.DeviceIdType.MESH
F32 = jnp.float32
BF16 = jnp.bfloat16
BS = 128
FWD_GROUP = 4
BWD_GROUP = 2
FWD_UNROLL = 4
BWD_UNROLL = 4
LIST_WIDTH = 384


def group_count(slots, keys, group, unroll):
    groups = (slots + keys * (group - 1)) // group
    return -(-groups // unroll) * unroll


def iota(shape, dim):
    return lax.broadcasted_iota(jnp.int32, shape, dim)


def sorted_lists(key, other, live, keys, group, groups):
    slots = key.shape[1]
    shift = group.bit_length() - 1
    picked = (iota((keys, slots), 0) == key) & live
    one_hot = jnp.where(picked, 1.0, 0.0).astype(F32)
    before = jnp.where(iota((slots, slots), 0) < iota((slots, slots), 1), 1.0, 0.0).astype(BF16)
    place = jnp.dot(one_hot.astype(BF16), before, preferred_element_type=F32)
    count = jnp.sum(one_hot, axis=1, keepdims=True).astype(jnp.int32)
    runs = lax.shift_right_logical(count + (group - 1), shift)
    lower = jnp.where(iota((keys, keys), 1) < iota((keys, keys), 0), 1.0, 0.0).astype(BF16)
    wide_runs = jnp.broadcast_to(runs, (keys, 128)).astype(F32).astype(BF16)
    start = jnp.dot(lower, wide_runs, preferred_element_type=F32)[:, :1]
    target = jnp.sum(one_hot * (start * group + place), axis=0, keepdims=True).astype(jnp.int32)
    target = jnp.where(live, target, -1)
    match = jnp.where(iota((LIST_WIDTH, slots), 0) == target, 1.0, 0.0).astype(BF16)
    number = iota((8, slots), 1)
    line = iota((8, slots), 0)
    facts = jnp.where(
        line == 0,
        lax.shift_right_logical(number, 4),
        jnp.where(line == 1, number & 15, jnp.where(line == 2, jnp.broadcast_to(other, (8, slots)), 1)),
    )
    found = lax.dot_general(
        facts.astype(F32).astype(BF16), match, (((1,), (1,)), ((), ())), preferred_element_type=F32
    ).astype(jnp.int32)
    slot = found[0:1] * 16 + found[1:2] + (1 - found[3:4]) * slots
    partner = found[2:3]
    start_int = start.astype(jnp.int32)
    lane = iota((keys, LIST_WIDTH), 1)
    opens = jnp.sum(jnp.where((start_int == lane) & (count > 0), 1.0, 0.0), axis=0, keepdims=True)
    keep = 1 - opens.astype(jnp.int32)
    final = jnp.where(count > 0, start_int + runs - 1, groups).astype(F32)
    last = jnp.sum(jnp.where(iota((keys, LIST_WIDTH), 0) == lane, final, 0.0), axis=0, keepdims=True)
    out_line = iota((8, LIST_WIDTH), 0)
    return jnp.where(
        out_line == 0,
        slot,
        jnp.where(out_line == 1, partner, jnp.where(out_line == 2, keep, last.astype(jnp.int32))),
    )


def lists_kernel(dims, rows_ref, cols_ref, live_ref, lists_ref):
    Z, X, Y, K = dims
    slots = rows_ref.shape[2]
    slab_blocks = 2 * Y * K
    col_blocks = 2 * Z * X
    live = iota((1, slots), 1) < live_ref[...]
    fwd_groups = group_count(slots, slab_blocks, FWD_GROUP, FWD_UNROLL)
    bwd_groups = group_count(slots, col_blocks, BWD_GROUP, BWD_UNROLL)
    lists_ref[0:8] = sorted_lists(rows_ref[0], cols_ref[0], live, slab_blocks, FWD_GROUP, fwd_groups)
    lists_ref[8:16] = sorted_lists(cols_ref[0], rows_ref[0], live, col_blocks, BWD_GROUP, bwd_groups)


def kernel(
    dims,
    scale,
    features_ref,
    weights_ref,
    bias_ref,
    values_hbm,
    lists,
    cotangent_ref,
    hidden_ref,
    grad_features_ref,
    grad_weights_ref,
    grad_bias_ref,
    values,
    panel,
    sums,
    core_out,
    core_in,
    y_out,
    y_in,
    agg_t,
    a_out,
    a_in,
    ax_out,
    ax_in,
    bx_out,
    bx_in,
    b_out,
    b_in,
    w_half,
    w_half_in,
    w_y,
    w_y_in,
    w_x,
    w_x_in,
    w_z,
    w_row,
    w_full,
    send_sem,
    recv_sem,
    local_sem,
):
    Z, X, Y, K = dims
    slots = values_hbm.shape[2]
    half_z = Z // 2
    half_x = X // 2
    slab_blocks = 2 * Y * K
    col_blocks = 2 * Z * X
    r = lax.axis_index("rows")
    c = lax.axis_index("rep")
    z, x, y, k = lax.div(r, X), lax.rem(r, X), lax.div(c, K), lax.rem(c, K)

    def at_z(step):
        return lax.rem(z + (step + Z), Z)

    def at_x(step):
        return lax.rem(x + (step + X), X)

    def at_y(step):
        return lax.rem(y + (step + Y), Y)

    def device(zz, xx, yy, kk):
        return (zz * X + xx, yy * K + kk)

    other_core = device(z, x, y, 1 - k)
    z_peers = [device(at_z(s), x, y, k) for s in range(1, Z)]
    x_peers = [device(z, at_x(s), y, k) for s in range(1, X)]
    y_peers = [device(z, x, at_y(s), k) for s in range(1, Y)]
    peers = [other_core] + z_peers + x_peers + y_peers

    barrier = pltpu.get_barrier_semaphore()
    for peer in peers:
        pl.semaphore_signal(barrier, inc=1, device_id=peer, device_id_type=MESH)

    load_values = pltpu.make_async_copy(
        values_hbm.at[0, 0], values.at[pl.ds(0, slots)], local_sem.at[0]
    )
    load_values.start()
    panel[2 * r] = features_ref[0:BS, :]
    panel[2 * r + 1] = features_ref[BS : 2 * BS, :]
    pl.semaphore_wait(barrier, len(peers))

    pending = []
    used = [0]

    def send(src, dst, to):
        i = used[0]
        used[0] += 1
        copy = pltpu.make_async_remote_copy(
            src_ref=src,
            dst_ref=dst,
            send_sem=send_sem.at[i],
            recv_sem=recv_sem.at[i],
            device_id=to,
            device_id_type=MESH,
        )
        copy.start()
        pending.append(copy)
        return copy

    def drain():
        for copy in pending:
            copy.wait_send()
        pending.clear()

    def share(piece, to):
        return send(piece, piece, to)

    up, down = device(at_z(1), x, y, k), device(at_z(-1), x, y, k)
    ways = ((1, up), (-1, down))
    halves = {1: pl.ds(0, BS // 2), -1: pl.ds(BS // 2, BS // 2)}
    x_steps = sorted(range(1, X), key=lambda d: -min(d, X - d))

    def shard(zz, xx, part):
        return panel.at[2 * (zz * X + xx) + part]

    a_x = {}
    for d in x_steps:
        a_x[d] = share(shard(z, x, 0), device(z, at_x(d), y, k))
    a_hop = {}
    b_hop = {}
    for s, to in ways:
        a_hop[s, 1, 0] = share(shard(z, x, 0), to)
        b_hop[s, 1] = share(shard(z, x, 1), to)
    b_x = []
    for d in x_steps:
        b_x.append(share(shard(z, x, 1), device(z, at_x(d), y, k)))

    values[slots] = jnp.zeros((BS, BS), BF16)
    fwd_groups = group_count(slots, slab_blocks, FWD_GROUP, FWD_UNROLL)
    bwd_groups = group_count(slots, col_blocks, BWD_GROUP, BWD_UNROLL)

    for d in reversed(x_steps):
        a_x[d].wait_recv()
        for s, to in ways:
            if half_z > 1 or (d < half_x) == (s > 0):
                a_hop[s, 1, d] = share(shard(z, at_x(-d), 0), to)
    for h in range(1, half_z + 1):
        for s, to in ways:
            b_hop[s, h].wait_recv()
            piece = shard(at_z(-s * h), x, 1)
            if h + 1 < half_z:
                b_hop[s, h + 1] = share(piece, to)
            elif h + 1 == half_z:
                b_hop[s, h + 1] = share(piece.at[halves[s]], to)
            for d in x_steps:
                part = piece.at[halves[s]] if h == half_z else piece
                b_x.append(share(part, device(z, at_x(d), y, k)))
        for d in range(X):
            for s, to in ways:
                if (s, h, d) in a_hop:
                    a_hop[s, h, d].wait_recv()
                    if h + 1 < half_z or (h + 1 == half_z and (d < half_x) == (s > 0)):
                        a_hop[s, h + 1, d] = share(shard(at_z(-s * h), at_x(-d), 0), to)
    for copy in b_x:
        copy.wait_recv()
    load_values.wait()

    zero_block = jnp.zeros((BS, BS), F32)

    def run_groups(line, group, groups, unroll, left, right):
        def step(base, total):
            for u in range(unroll):
                t = base * unroll + u
                at = t * group
                lhs = [left(at + g) for g in range(group)]
                rhs = [right(at + g) for g in range(group)]
                product = jnp.dot(
                    jnp.concatenate(lhs, axis=1),
                    jnp.concatenate(rhs, axis=0),
                    preferred_element_type=F32,
                )
                total = product + total * lists[line + 2, t].astype(F32)
                sums[t] = total
            return total

        assert groups % unroll == 0
        lax.fori_loop(0, groups // unroll, step, zero_block)
        sums[groups] = zero_block

    run_groups(
        0,
        FWD_GROUP,
        fwd_groups,
        FWD_UNROLL,
        lambda at: values[lists[0, at]],
        lambda at: panel[lists[1, at]],
    )

    def row_pair(yy, kk, i):
        return sums[lists[3, 2 * (yy * K + kk) + i]]

    y_steps = sorted(range(1, Y), key=lambda d: -min(d, Y - d))
    from_core = {}
    for d in y_steps + [0]:
        for i in range(2):
            core_out[d, i] = row_pair(at_y(d), 1 - k, i).astype(BF16)
        from_core[d] = send(core_out.at[d], core_in.at[d], other_core)
    from_y = {}
    for d in y_steps:
        from_core[d].wait_recv()
        for i in range(2):
            y_out[d, i] = (row_pair(at_y(d), k, i) + core_in[d, i].astype(F32)).astype(BF16)
        from_y[d] = send(y_out.at[d], y_in.at[d], device(z, x, at_y(d), k))
    from_core[0].wait_recv()
    own = [row_pair(y, k, i) + core_in[0, i].astype(F32) for i in range(2)]
    for d in y_steps:
        from_y[d].wait_recv()
        for i in range(2):
            own[i] = own[i] + y_in[d, i].astype(F32)
    aggregate = jnp.concatenate(own, axis=0).astype(BF16)

    weights = weights_ref[...]
    preact = jnp.dot(aggregate, weights, preferred_element_type=F32) + bias_ref[...]
    sigma = 1.0 / (1.0 + jnp.exp(-preact))
    deriv = sigma * (1.0 + preact * (1.0 - sigma))
    grad_pre_wide = cotangent_ref[...].astype(F32) * deriv
    grad_pre = grad_pre_wide.astype(BF16)
    grad_t = lax.dot_general(
        weights, grad_pre, (((1,), (1,)), ((), ())), preferred_element_type=F32
    ).astype(BF16)
    agg_t[2 * c] = grad_t[:, 0:BS]
    agg_t[2 * c + 1] = grad_t[:, BS : 2 * BS]

    def slab_pair(yy, kk):
        return agg_t.at[pl.ds(2 * (yy * K + kk), 2)]

    from_y = {}
    for d in y_steps:
        from_y[d] = share(slab_pair(y, k), device(z, x, at_y(d), k))
    from_core = [share(slab_pair(y, k), other_core)]
    hidden_ref[...] = (preact * sigma).astype(BF16)
    weight_term = lax.dot_general(
        aggregate, grad_pre, (((0,), (0,)), ((), ())), preferred_element_type=F32
    )
    bias_term = jnp.sum(grad_pre.astype(F32), axis=0, keepdims=True)
    grad_weights_ref[...] = weight_term
    rows_core = BS // K
    rows_y = rows_core // Y
    w_tall = rows_y + 8
    rows_x = w_z.shape[1]

    def rows_at(start, size):
        return pl.ds(pl.multiple_of(start, 8), size)

    for i, kk in ((0, 1 - k), (1, k)):
        w_half[i, 0:rows_core] = grad_weights_ref[rows_at(kk * rows_core, rows_core), :]
        w_half[i, rows_core : rows_core + 8] = jnp.broadcast_to(bias_term, (8, bias_term.shape[1]))
    w_core = send(w_half.at[0], w_half_in, other_core)
    for d in reversed(y_steps):
        from_y[d].wait_recv()
        from_core.append(share(slab_pair(at_y(-d), k), other_core))
    w_core.wait_recv()
    w_half[1] = w_half[1] + w_half_in[...]
    bias_rows = w_half[1, rows_core : rows_core + 8]
    w_from_y = []
    for d in range(Y):
        w_y[d, 0:rows_y] = w_half[1, rows_at(at_y(d) * rows_y, rows_y), :]
        w_y[d, rows_y:w_tall] = bias_rows
    for d in y_steps:
        w_from_y.append(send(w_y.at[d], w_y_in.at[y], device(z, x, at_y(d), k)))
    w_y_in[y] = w_y[0]
    drain()
    for copy in from_core:
        copy.wait_recv()

    run_groups(
        8,
        BWD_GROUP,
        bwd_groups,
        BWD_UNROLL,
        lambda at: agg_t[lists[9, at]],
        lambda at: values[lists[8, at]],
    )

    def column(zz, xx, part):
        return sums[lists[11, 2 * (zz * X + xx) + part]]

    w_copies = {}

    def stage_x():
        for copy in w_from_y:
            copy.wait_recv()
        total = w_y_in[0]
        for yy in range(1, Y):
            total = total + w_y_in[yy]
        w_x[0:w_tall] = total
        if rows_x * X > w_tall:
            w_x[w_tall : rows_x * X] = jnp.zeros((rows_x * X - w_tall, total.shape[1]), F32)
        w_copies["x"] = [
            send(w_x.at[rows_at(at_x(d) * rows_x, rows_x)], w_x_in.at[x], device(z, at_x(d), y, k))
            for d in x_steps
        ]
        w_x_in[x] = w_x[rows_at(x * rows_x, rows_x), :]

    def stage_z():
        for copy in w_copies["x"]:
            copy.wait_recv()
        total = w_x_in[0]
        for xx in range(1, X):
            total = total + w_x_in[xx]
        w_z[z] = total
        w_copies["z"] = [share(w_z.at[z], peer) for peer in z_peers]

    def stage_back_x():
        for copy in w_copies["z"]:
            copy.wait_recv()
        total = w_z[0]
        for zz in range(1, Z):
            total = total + w_z[zz]
        w_row[rows_at(x * rows_x, rows_x), :] = total
        w_copies["bx"] = [
            share(w_row.at[rows_at(x * rows_x, rows_x)], device(z, at_x(d), y, k)) for d in x_steps
        ]

    def stage_back_y():
        for copy in w_copies["bx"]:
            copy.wait_recv()
        mine = rows_at(k * rows_core + y * rows_y, rows_y)
        w_full[mine, :] = w_row[0:rows_y]
        w_copies["by"] = [share(w_full.at[mine], device(z, x, at_y(d), k)) for d in y_steps]

    def stage_back_core():
        for copy in w_copies["by"]:
            copy.wait_recv()
        mine = rows_at(k * rows_core, rows_core)
        w_copies["bc"] = [share(w_full.at[mine], other_core)]

    stages = [stage_z, stage_back_x, stage_back_y, stage_back_core]

    a_hop = {}
    b_hop = {}
    b_x = {}

    def send_a(s, to, h, d):
        if h == 1 and (d < half_x) != (s > 0):
            return
        total = column(at_z(s * (half_z - h + 1)), at_x(d), 0)
        if (s, h - 1, d) in a_hop:
            a_hop[s, h - 1, d].wait_recv()
            total = total + a_in[way_of[s], h - 2, d].astype(F32)
        a_out[way_of[s], h - 1, d] = total.astype(BF16)
        a_hop[s, h, d] = send(a_out.at[way_of[s], h - 1, d], a_in.at[way_of[s], h - 1, d], to)

    way_of = {1: 0, -1: 1}

    def send_bx(dz):
        for d in x_steps:
            bx_out[d, dz % Z] = column(at_z(dz), at_x(d), 1).astype(BF16)
            b_x[d, dz] = send(
                bx_out.at[d, dz % Z], bx_in.at[d, dz % Z], device(z, at_x(d), y, k)
            )

    def sum_bx(dz):
        total = column(at_z(dz), x, 1)
        for d in x_steps:
            b_x[d, dz].wait_recv()
            total = total + bx_in[d, dz % Z].astype(F32)
        return total

    for d in range(X):
        for s, to in ways:
            send_a(s, to, 1, d)
    send_bx(half_z)
    for far in range(half_z - 1, 0, -1):
        send_bx(far)
        send_bx(-far)
    send_bx(0)
    stage_x()
    for h in range(2, half_z + 1):
        for d in range(X):
            for s, to in ways:
                send_a(s, to, h, d)
        if h == 2:
            total = sum_bx(half_z)
            for s, to in ways:
                i = way_of[s]
                rows = slice(0, BS // 2) if s > 0 else slice(BS // 2, BS)
                b_out[i, 0, halves[s]] = total[rows].astype(BF16)
                b_hop[s, 1] = send(b_out.at[i, 0, halves[s]], b_in.at[i, 0, halves[s]], to)
        else:
            for s, to in ways:
                i = way_of[s]
                total = sum_bx(s * (half_z - h + 2))
                b_hop[s, h - 2].wait_recv()
                if h == 3:
                    rows = slice(0, BS // 2) if s > 0 else slice(BS // 2, BS)
                    top, low = total[0 : BS // 2], total[BS // 2 : BS]
                    got = b_in[i, 0, halves[s]].astype(F32)
                    if s > 0:
                        top = top + got
                    else:
                        low = low + got
                    total = jnp.concatenate([top, low], axis=0)
                else:
                    total = total + b_in[i, h - 3].astype(F32)
                b_out[i, h - 2] = total.astype(BF16)
                b_hop[s, h - 1] = send(b_out.at[i, h - 2], b_in.at[i, h - 2], to)
        if stages:
            stages.pop(0)()
    last_a = []
    from_x = {}
    for d in x_steps + [0]:
        total = column(z, at_x(d), 0)
        for s, _ in ways:
            if (s, half_z, d) in a_hop:
                a_hop[s, half_z, d].wait_recv()
                total = total + a_in[way_of[s], half_z - 1, d].astype(F32)
        if d:
            ax_out[d] = total.astype(BF16)
            from_x[d] = send(ax_out.at[d], ax_in.at[d], device(z, at_x(d), y, k))
        else:
            last_a = total
    for s, to in ways:
        i = way_of[s]
        h = half_z + 1
        total = sum_bx(s)
        b_hop[s, h - 2].wait_recv()
        if h == 3:
            top, low = total[0 : BS // 2], total[BS // 2 : BS]
            got = b_in[i, 0, halves[s]].astype(F32)
            if s > 0:
                top = top + got
            else:
                low = low + got
            total = jnp.concatenate([top, low], axis=0)
        else:
            total = total + b_in[i, h - 3].astype(F32)
        b_out[i, h - 2] = total.astype(BF16)
        b_hop[s, h - 1] = send(b_out.at[i, h - 2], b_in.at[i, h - 2], to)
    while stages:
        stages.pop(0)()
    last_b = sum_bx(0)
    for d in x_steps:
        from_x[d].wait_recv()
        last_a = last_a + ax_in[d].astype(F32)
    grad_features_ref[0:BS, :] = last_a.T
    grad_bias_ref[...] = w_row[rows_y : rows_y + 1] * scale
    drain()
    for s, _ in ways:
        b_hop[s, half_z].wait_recv()
        last_b = last_b + b_in[way_of[s], half_z - 1].astype(F32)
    grad_features_ref[BS : 2 * BS, :] = last_b.T
    w_copies["bc"][0].wait_recv()
    grad_weights_ref[...] = w_full[...] * scale


def mesh_dims(mesh):
    rows, rep = mesh.shape["rows"], mesh.shape["rep"]
    across = 4 if rows >= 32 else 2
    return rows // across, across, rep // 2, 2


def shards(
    dims, features, weights, bias_vector, block_values, block_rows, block_cols, block_live, cotangent
):
    Z, X, Y, K = dims
    nodes, width = features.shape
    hid = weights.shape[1]
    slots = block_values.shape[2]
    half_z = Z // 2
    groups = max(
        group_count(slots, 2 * Y * K, FWD_GROUP, FWD_UNROLL),
        group_count(slots, 2 * Z * X, BWD_GROUP, BWD_UNROLL),
    )
    rows_y = BS // K // Y
    rows_x = -(-(rows_y + 8) // (8 * X)) * 8
    scale = 1.0 / math.sqrt(nodes * Z * X * Y * K)
    copies = 400
    vmem = pl.BlockSpec(memory_space=pltpu.VMEM)
    block = (BS, BS)
    lists = pl.pallas_call(
        functools.partial(lists_kernel, dims),
        out_shape=jax.ShapeDtypeStruct((16, LIST_WIDTH), jnp.int32),
        in_specs=[vmem, vmem, vmem],
        out_specs=vmem,
        name="lists",
    )(block_rows, block_cols, block_live)
    out = pl.pallas_call(
        functools.partial(kernel, dims, scale),
        out_shape=(
            jax.ShapeDtypeStruct((nodes, hid), BF16),
            jax.ShapeDtypeStruct((nodes, width), F32),
            jax.ShapeDtypeStruct((width, hid), F32),
            jax.ShapeDtypeStruct((1, hid), F32),
        ),
        in_specs=[
            vmem,
            vmem,
            vmem,
            pl.BlockSpec(memory_space=pl.ANY),
            pl.BlockSpec(memory_space=pltpu.SMEM),
            vmem,
        ],
        out_specs=(vmem, vmem, vmem, vmem),
        scratch_shapes=[
            pltpu.VMEM((slots + 1, *block), BF16),
            pltpu.VMEM((2 * Z * X, *block), BF16),
            pltpu.VMEM((groups + 1, *block), F32),
            pltpu.VMEM((Y, 2, *block), BF16),
            pltpu.VMEM((Y, 2, *block), BF16),
            pltpu.VMEM((Y, 2, *block), BF16),
            pltpu.VMEM((Y, 2, *block), BF16),
            pltpu.VMEM((2 * Y * K, *block), BF16),
            pltpu.VMEM((2, half_z, X, *block), BF16),
            pltpu.VMEM((2, half_z, X, *block), BF16),
            pltpu.VMEM((X, *block), BF16),
            pltpu.VMEM((X, *block), BF16),
            pltpu.VMEM((X, Z, *block), BF16),
            pltpu.VMEM((X, Z, *block), BF16),
            pltpu.VMEM((2, half_z, *block), BF16),
            pltpu.VMEM((2, half_z, *block), BF16),
            pltpu.VMEM((2, BS // K + 8, hid), F32),
            pltpu.VMEM((BS // K + 8, hid), F32),
            pltpu.VMEM((Y, rows_y + 8, hid), F32),
            pltpu.VMEM((Y, rows_y + 8, hid), F32),
            pltpu.VMEM((rows_x * X, hid), F32),
            pltpu.VMEM((X, rows_x, hid), F32),
            pltpu.VMEM((Z, rows_x, hid), F32),
            pltpu.VMEM((rows_x * X, hid), F32),
            pltpu.VMEM((BS, hid), F32),
            pltpu.SemaphoreType.DMA((copies,)),
            pltpu.SemaphoreType.DMA((copies,)),
            pltpu.SemaphoreType.DMA((1,)),
        ],
        compiler_params=pltpu.CompilerParams(
            collective_id=0, has_side_effects=True, vmem_limit_bytes=52 * 1024 * 1024
        ),
        name="layer",
    )(
        features,
        weights,
        bias_vector.reshape(1, hid),
        block_values,
        lists,
        cotangent,
    )
    hidden, grad_features, grad_weights, grad_bias = out
    return hidden, grad_features, grad_weights, grad_bias.reshape(hid)


def solution(mesh):
    in_specs = (
        P(("rows", "rep"), None),
        P(),
        P(),
        P("rows", "rep", None, None, None),
        P("rows", "rep", None),
        P("rows", "rep", None),
        P("rows", "rep"),
        P(("rows", "rep"), None),
    )
    out_specs = (P(("rows", "rep"), None), P(("rows", "rep"), None), P(), P())
    return jax.shard_map(
        functools.partial(shards, mesh_dims(mesh)),
        mesh=mesh,
        in_specs=in_specs,
        out_specs=out_specs,
        check_vma=False,
    )
```

```python
import functools
import math

import jax
import jax.numpy as jnp
from jax import lax
from jax.experimental import pallas as pl
from jax.experimental.pallas import tpu as pltpu
from jax.sharding import PartitionSpec as P

MESH = pl.DeviceIdType.MESH
F32 = jnp.float32
BF16 = jnp.bfloat16
BS = 128
FWD_GROUP = 4
BWD_GROUP = 2
FWD_UNROLL = 23
BWD_UNROLL = 32
BWD_PARTS = 3
SEND_SLOTS = 84
RECV_SLOTS = 164
LIST_WIDTH = 384


def group_count(slots, keys, group, unroll):
    groups = (slots + keys * (group - 1)) // group
    return -(-groups // unroll) * unroll


def iota(shape, dim):
    return lax.broadcasted_iota(jnp.int32, shape, dim)


def sorted_lists(key, other, live, keys, group, groups):
    slots = key.shape[1]
    shift = group.bit_length() - 1
    picked = (iota((keys, slots), 0) == key) & live
    one_hot = jnp.where(picked, 1.0, 0.0).astype(F32)
    before = jnp.where(iota((slots, slots), 0) < iota((slots, slots), 1), 1.0, 0.0).astype(BF16)
    place = jnp.dot(one_hot.astype(BF16), before, preferred_element_type=F32)
    count = jnp.sum(one_hot, axis=1, keepdims=True).astype(jnp.int32)
    runs = lax.shift_right_logical(count + (group - 1), shift)
    lower = jnp.where(iota((keys, keys), 1) < iota((keys, keys), 0), 1.0, 0.0).astype(BF16)
    wide_runs = jnp.broadcast_to(runs, (keys, 128)).astype(F32).astype(BF16)
    start = jnp.dot(lower, wide_runs, preferred_element_type=F32)[:, :1]
    target = jnp.sum(one_hot * (start * group + place), axis=0, keepdims=True).astype(jnp.int32)
    target = jnp.where(live, target, -1)
    match = jnp.where(iota((LIST_WIDTH, slots), 0) == target, 1.0, 0.0).astype(BF16)
    number = iota((8, slots), 1)
    line = iota((8, slots), 0)
    facts = jnp.where(
        line == 0,
        lax.shift_right_logical(number, 4),
        jnp.where(line == 1, number & 15, jnp.where(line == 2, jnp.broadcast_to(other, (8, slots)), 1)),
    )
    found = lax.dot_general(
        facts.astype(F32).astype(BF16), match, (((1,), (1,)), ((), ())), preferred_element_type=F32
    ).astype(jnp.int32)
    slot = found[0:1] * 16 + found[1:2] + (1 - found[3:4]) * slots
    partner = found[2:3]
    start_int = start.astype(jnp.int32)
    lane = iota((keys, LIST_WIDTH), 1)
    opens = jnp.sum(jnp.where((start_int == lane) & (count > 0), 1.0, 0.0), axis=0, keepdims=True)
    keep = 1 - opens.astype(jnp.int32)
    final = jnp.where(count > 0, start_int + runs - 1, groups).astype(F32)
    last = jnp.sum(jnp.where(iota((keys, LIST_WIDTH), 0) == lane, final, 0.0), axis=0, keepdims=True)
    out_line = iota((8, LIST_WIDTH), 0)
    return jnp.where(
        out_line == 0,
        slot,
        jnp.where(out_line == 1, partner, jnp.where(out_line == 2, keep, last.astype(jnp.int32))),
    )


def lists_kernel(dims, rows_hbm, cols_hbm, live_ref, lists_ref, rows_ref, cols_ref, sem):
    copies = [
        pltpu.make_async_copy(rows_hbm, rows_ref, sem.at[0]),
        pltpu.make_async_copy(cols_hbm, cols_ref, sem.at[1]),
    ]
    for copy in copies:
        copy.start()
    for copy in copies:
        copy.wait()
    Z, X, Y, K = dims
    slots = rows_ref.shape[2]
    slab_blocks = 2 * Y * K
    col_blocks = 2 * Z * X
    live = iota((1, slots), 1) < live_ref[...]
    fwd_groups = group_count(slots, slab_blocks, FWD_GROUP, FWD_UNROLL)
    bwd_groups = group_count(slots, col_blocks, BWD_GROUP, BWD_PARTS * BWD_UNROLL)
    lists_ref[0:8] = sorted_lists(rows_ref[0], cols_ref[0], live, slab_blocks, FWD_GROUP, fwd_groups)
    lists_ref[8:16] = sorted_lists(cols_ref[0], rows_ref[0], live, col_blocks, BWD_GROUP, bwd_groups)


def kernel(
    dims,
    scale,
    features_hbm,
    weights_hbm,
    bias_hbm,
    values_hbm,
    lists_hbm,
    cotangent_hbm,
    hidden_ref,
    grad_features_ref,
    grad_weights_ref,
    grad_bias_ref,
    lists,
    values,
    weights_ref,
    bias_ref,
    cotangent_ref,
    panel,
    sums,
    core_out,
    core_in,
    y_out,
    y_in,
    agg_t,
    a_out,
    a_in,
    ax_out,
    ax_in,
    bx_out,
    bx_in,
    b_out,
    b_in,
    w_half,
    w_half_in,
    w_y,
    w_y_in,
    w_x,
    w_x_in,
    w_z,
    w_row,
    w_full,
    send_sem,
    recv_sem,
    local_sem,
):
    Z, X, Y, K = dims
    slots = values_hbm.shape[2]
    half_z = Z // 2
    half_x = X // 2
    slab_blocks = 2 * Y * K
    col_blocks = 2 * Z * X
    r = lax.axis_index("rows")
    c = lax.axis_index("rep")
    z, x, y, k = lax.div(r, X), lax.rem(r, X), lax.div(c, K), lax.rem(c, K)

    def at_z(step):
        return lax.rem(z + (step + Z), Z)

    def at_x(step):
        return lax.rem(x + (step + X), X)

    def at_y(step):
        return lax.rem(y + (step + Y), Y)

    def device(zz, xx, yy, kk):
        return (zz * X + xx, yy * K + kk)

    other_core = device(z, x, y, 1 - k)
    z_peers = [device(at_z(s), x, y, k) for s in range(1, Z)]
    x_peers = [device(z, at_x(s), y, k) for s in range(1, X)]
    y_peers = [device(z, x, at_y(s), k) for s in range(1, Y)]
    peers = [other_core] + z_peers + x_peers + y_peers

    barrier = pltpu.get_barrier_semaphore()
    for peer in peers:
        pl.semaphore_signal(barrier, inc=1, device_id=peer, device_id_type=MESH)

    load_values = pltpu.make_async_copy(
        values_hbm.at[0, 0], values.at[pl.ds(0, slots)], local_sem.at[0]
    )
    load_own = [
        pltpu.make_async_copy(
            features_hbm.at[pl.ds(i * BS, BS)], panel.at[2 * r + i], local_sem.at[1 + i]
        )
        for i in range(2)
    ]
    for copy in load_own:
        copy.start()
    load_values.start()
    load_layer = [
        pltpu.make_async_copy(weights_hbm, weights_ref, local_sem.at[3]),
        pltpu.make_async_copy(bias_hbm, bias_ref, local_sem.at[4]),
        pltpu.make_async_copy(cotangent_hbm, cotangent_ref, local_sem.at[5]),
    ]
    for copy in load_layer:
        copy.start()
    load_lists = pltpu.make_async_copy(lists_hbm, lists, local_sem.at[6])
    load_lists.start()
    pl.semaphore_wait(barrier, len(peers))
    for copy in load_own:
        copy.wait()

    pending = []
    used = [0]

    def send(src, dst, to):
        i = used[0]
        used[0] += 1
        free = len(pending)
        copy = pltpu.make_async_remote_copy(
            src_ref=src,
            dst_ref=dst,
            send_sem=send_sem.at[free],
            recv_sem=recv_sem.at[i],
            device_id=to,
            device_id_type=MESH,
        )
        copy.start()
        pending.append(copy)
        return copy

    def drain():
        for copy in pending:
            copy.wait_send()
        pending.clear()

    def share(piece, to):
        return send(piece, piece, to)

    up, down = device(at_z(1), x, y, k), device(at_z(-1), x, y, k)
    ways = ((1, up), (-1, down))
    halves = {1: pl.ds(0, BS // 2), -1: pl.ds(BS // 2, BS // 2)}
    x_steps = sorted(range(1, X), key=lambda d: -min(d, X - d))

    def shard(zz, xx, part):
        return panel.at[2 * (zz * X + xx) + part]

    a_x = {}
    for d in x_steps:
        a_x[d] = share(shard(z, x, 0), device(z, at_x(d), y, k))
    a_hop = {}
    b_hop = {}
    for s, to in ways:
        a_hop[s, 1, 0] = share(shard(z, x, 0), to)
        b_hop[s, 1] = share(shard(z, x, 1), to)
    b_x = []
    for d in x_steps:
        b_x.append(share(shard(z, x, 1), device(z, at_x(d), y, k)))

    values[slots] = jnp.zeros((BS, BS), BF16)
    fwd_groups = group_count(slots, slab_blocks, FWD_GROUP, FWD_UNROLL)
    bwd_groups = group_count(slots, col_blocks, BWD_GROUP, BWD_PARTS * BWD_UNROLL)

    for d in reversed(x_steps):
        a_x[d].wait_recv()
        for s, to in ways:
            if half_z > 1 or (d < half_x) == (s > 0):
                a_hop[s, 1, d] = share(shard(z, at_x(-d), 0), to)
    for h in range(1, half_z + 1):
        for s, to in ways:
            b_hop[s, h].wait_recv()
            piece = shard(at_z(-s * h), x, 1)
            if h + 1 < half_z:
                b_hop[s, h + 1] = share(piece, to)
            elif h + 1 == half_z:
                b_hop[s, h + 1] = share(piece.at[halves[s]], to)
            for d in x_steps:
                part = piece.at[halves[s]] if h == half_z else piece
                b_x.append(share(part, device(z, at_x(d), y, k)))
        for d in range(X):
            for s, to in ways:
                if (s, h, d) in a_hop:
                    a_hop[s, h, d].wait_recv()
                    if h + 1 < half_z or (h + 1 == half_z and (d < half_x) == (s > 0)):
                        a_hop[s, h + 1, d] = share(shard(at_z(-s * h), at_x(-d), 0), to)
    for copy in b_x:
        copy.wait_recv()
    load_lists.wait()
    load_values.wait()

    zero_block = jnp.zeros((BS, BS), F32)

    def run_groups(line, group, first, groups, unroll, left, right, total):
        def step(base, total):
            for u in range(unroll):
                t = first + base * unroll + u
                at = t * group
                lhs = [left(at + g) for g in range(group)]
                rhs = [right(at + g) for g in range(group)]
                product = jnp.dot(
                    jnp.concatenate(lhs, axis=1),
                    jnp.concatenate(rhs, axis=0),
                    preferred_element_type=F32,
                )
                total = product + total * lists[line + 2, t].astype(F32)
                sums[t] = total
            return total

        assert groups % unroll == 0
        return lax.fori_loop(0, groups // unroll, step, total)

    run_groups(
        0,
        FWD_GROUP,
        0,
        fwd_groups,
        FWD_UNROLL,
        lambda at: values[lists[0, at]],
        lambda at: panel[lists[1, at]],
        zero_block,
    )
    sums[fwd_groups] = zero_block

    def row_pair(yy, kk, i):
        return sums[lists[3, 2 * (yy * K + kk) + i]]

    y_steps = sorted(range(1, Y), key=lambda d: -min(d, Y - d))
    from_core = {}
    for d in y_steps + [0]:
        for i in range(2):
            core_out[d, i] = row_pair(at_y(d), 1 - k, i).astype(BF16)
        from_core[d] = send(core_out.at[d], core_in.at[d], other_core)
    from_y = {}
    for d in y_steps:
        from_core[d].wait_recv()
        for i in range(2):
            y_out[d, i] = (row_pair(at_y(d), k, i) + core_in[d, i].astype(F32)).astype(BF16)
        from_y[d] = send(y_out.at[d], y_in.at[d], device(z, x, at_y(d), k))
    from_core[0].wait_recv()
    own = [row_pair(y, k, i) + core_in[0, i].astype(F32) for i in range(2)]
    for d in y_steps:
        from_y[d].wait_recv()
        for i in range(2):
            own[i] = own[i] + y_in[d, i].astype(F32)
    aggregate = jnp.concatenate(own, axis=0).astype(BF16)

    for copy in load_layer:
        copy.wait()
    weights = weights_ref[...]
    preact = jnp.dot(aggregate, weights, preferred_element_type=F32) + bias_ref[...]
    sigma = 1.0 / (1.0 + jnp.exp(-preact))
    deriv = sigma * (1.0 + preact * (1.0 - sigma))
    grad_pre_wide = cotangent_ref[...].astype(F32) * deriv
    grad_pre = grad_pre_wide.astype(BF16)
    grad_t = lax.dot_general(
        weights, grad_pre, (((1,), (1,)), ((), ())), preferred_element_type=F32
    ).astype(BF16)
    agg_t[2 * c] = grad_t[:, 0:BS]
    agg_t[2 * c + 1] = grad_t[:, BS : 2 * BS]

    def slab_pair(yy, kk):
        return agg_t.at[pl.ds(2 * (yy * K + kk), 2)]

    from_y = {}
    for d in y_steps:
        from_y[d] = share(slab_pair(y, k), device(z, x, at_y(d), k))
    from_core = [share(slab_pair(y, k), other_core)]
    hidden_ref[...] = (preact * sigma).astype(BF16)
    weight_term = lax.dot_general(
        aggregate, grad_pre, (((0,), (0,)), ((), ())), preferred_element_type=F32
    )
    bias_term = jnp.sum(grad_pre.astype(F32), axis=0, keepdims=True)
    grad_weights_ref[...] = weight_term
    rows_core = BS // K
    rows_y = rows_core // Y
    w_tall = rows_y + 8
    rows_x = w_z.shape[1]

    def rows_at(start, size):
        return pl.ds(pl.multiple_of(start, 8), size)

    for i, kk in ((0, 1 - k), (1, k)):
        w_half[i, 0:rows_core] = grad_weights_ref[rows_at(kk * rows_core, rows_core), :]
        w_half[i, rows_core : rows_core + 8] = jnp.broadcast_to(bias_term, (8, bias_term.shape[1]))
    w_core = send(w_half.at[0], w_half_in, other_core)
    for d in reversed(y_steps):
        from_y[d].wait_recv()
        from_core.append(share(slab_pair(at_y(-d), k), other_core))
    w_core.wait_recv()
    w_half[1] = w_half[1] + w_half_in[...]
    bias_rows = w_half[1, rows_core : rows_core + 8]
    w_from_y = []
    for d in range(Y):
        w_y[d, 0:rows_y] = w_half[1, rows_at(at_y(d) * rows_y, rows_y), :]
        w_y[d, rows_y:w_tall] = bias_rows
    for d in y_steps:
        w_from_y.append(send(w_y.at[d], w_y_in.at[y], device(z, x, at_y(d), k)))
    w_y_in[y] = w_y[0]
    drain()
    for copy in from_core:
        copy.wait_recv()

    w_copies = {}

    def stage_x():
        for copy in w_from_y:
            copy.wait_recv()
        total = w_y_in[0]
        for yy in range(1, Y):
            total = total + w_y_in[yy]
        w_x[0:w_tall] = total
        if rows_x * X > w_tall:
            w_x[w_tall : rows_x * X] = jnp.zeros((rows_x * X - w_tall, total.shape[1]), F32)
        w_copies["x"] = [
            send(w_x.at[rows_at(at_x(d) * rows_x, rows_x)], w_x_in.at[x], device(z, at_x(d), y, k))
            for d in x_steps
        ]
        w_x_in[x] = w_x[rows_at(x * rows_x, rows_x), :]

    def stage_z():
        for copy in w_copies["x"]:
            copy.wait_recv()
        total = w_x_in[0]
        for xx in range(1, X):
            total = total + w_x_in[xx]
        w_z[z] = total
        w_copies["z"] = [share(w_z.at[z], peer) for peer in z_peers]

    def stage_back_x():
        for copy in w_copies["z"]:
            copy.wait_recv()
        total = w_z[0]
        for zz in range(1, Z):
            total = total + w_z[zz]
        w_row[rows_at(x * rows_x, rows_x), :] = total
        w_copies["bx"] = [
            share(w_row.at[rows_at(x * rows_x, rows_x)], device(z, at_x(d), y, k)) for d in x_steps
        ]

    def stage_back_y():
        for copy in w_copies["bx"]:
            copy.wait_recv()
        mine = rows_at(k * rows_core + y * rows_y, rows_y)
        w_full[mine, :] = w_row[0:rows_y]
        w_copies["by"] = [share(w_full.at[mine], device(z, x, at_y(d), k)) for d in y_steps]

    def stage_back_core():
        for copy in w_copies["by"]:
            copy.wait_recv()
        mine = rows_at(k * rows_core, rows_core)
        w_copies["bc"] = [share(w_full.at[mine], other_core)]

    stages = [stage_back_y, stage_back_core]

    part_groups = bwd_groups // BWD_PARTS
    running = zero_block
    for part in range(BWD_PARTS):
        running = run_groups(
            8,
            BWD_GROUP,
            part * part_groups,
            part_groups,
            BWD_UNROLL,
            lambda at: agg_t[lists[9, at]],
            lambda at: values[lists[8, at]],
            running,
        )
        if part < 2:
            (stage_x, stage_z)[part]()
    sums[bwd_groups] = zero_block

    def column(zz, xx, part):
        return sums[lists[11, 2 * (zz * X + xx) + part]]

    a_hop = {}
    b_hop = {}
    b_x = {}

    def send_a(s, to, h, d):
        if h == 1 and (d < half_x) != (s > 0):
            return
        total = column(at_z(s * (half_z - h + 1)), at_x(d), 0)
        if (s, h - 1, d) in a_hop:
            a_hop[s, h - 1, d].wait_recv()
            total = total + a_in[way_of[s], h - 2, d].astype(F32)
        a_out[way_of[s], h - 1, d] = total.astype(BF16)
        a_hop[s, h, d] = send(a_out.at[way_of[s], h - 1, d], a_in.at[way_of[s], h - 1, d], to)

    way_of = {1: 0, -1: 1}

    def send_bx(dz):
        for d in x_steps:
            bx_out[d, dz % Z] = column(at_z(dz), at_x(d), 1).astype(BF16)
            b_x[d, dz] = send(
                bx_out.at[d, dz % Z], bx_in.at[d, dz % Z], device(z, at_x(d), y, k)
            )

    def sum_bx(dz):
        total = column(at_z(dz), x, 1)
        for d in x_steps:
            b_x[d, dz].wait_recv()
            total = total + bx_in[d, dz % Z].astype(F32)
        return total

    for d in range(X):
        for s, to in ways:
            send_a(s, to, 1, d)
    send_bx(half_z)
    for far in range(half_z - 1, 0, -1):
        send_bx(far)
        send_bx(-far)
        if far == half_z - 1:
            stage_back_x()
    send_bx(0)
    for h in range(2, half_z + 1):
        for d in range(X):
            for s, to in ways:
                send_a(s, to, h, d)
        if h == 2:
            total = sum_bx(half_z)
            for s, to in ways:
                i = way_of[s]
                rows = slice(0, BS // 2) if s > 0 else slice(BS // 2, BS)
                b_out[i, 0, halves[s]] = total[rows].astype(BF16)
                b_hop[s, 1] = send(b_out.at[i, 0, halves[s]], b_in.at[i, 0, halves[s]], to)
        else:
            for s, to in ways:
                i = way_of[s]
                total = sum_bx(s * (half_z - h + 2))
                b_hop[s, h - 2].wait_recv()
                if h == 3:
                    rows = slice(0, BS // 2) if s > 0 else slice(BS // 2, BS)
                    top, low = total[0 : BS // 2], total[BS // 2 : BS]
                    got = b_in[i, 0, halves[s]].astype(F32)
                    if s > 0:
                        top = top + got
                    else:
                        low = low + got
                    total = jnp.concatenate([top, low], axis=0)
                else:
                    total = total + b_in[i, h - 3].astype(F32)
                b_out[i, h - 2] = total.astype(BF16)
                b_hop[s, h - 1] = send(b_out.at[i, h - 2], b_in.at[i, h - 2], to)
        if stages:
            stages.pop(0)()
    last_a = None
    from_x = {}
    for d in x_steps + [0]:
        total = column(z, at_x(d), 0)
        for s, _ in ways:
            if (s, half_z, d) in a_hop:
                a_hop[s, half_z, d].wait_recv()
                total = total + a_in[way_of[s], half_z - 1, d].astype(F32)
        if d:
            ax_out[d] = total.astype(BF16)
            from_x[d] = send(ax_out.at[d], ax_in.at[d], device(z, at_x(d), y, k))
        else:
            last_a = total
    for s, to in ways:
        i = way_of[s]
        h = half_z + 1
        total = sum_bx(s)
        b_hop[s, h - 2].wait_recv()
        if h == 3:
            top, low = total[0 : BS // 2], total[BS // 2 : BS]
            got = b_in[i, 0, halves[s]].astype(F32)
            if s > 0:
                top = top + got
            else:
                low = low + got
            total = jnp.concatenate([top, low], axis=0)
        else:
            total = total + b_in[i, h - 3].astype(F32)
        b_out[i, h - 2] = total.astype(BF16)
        b_hop[s, h - 1] = send(b_out.at[i, h - 2], b_in.at[i, h - 2], to)
    while stages:
        stages.pop(0)()
    last_b = sum_bx(0)
    for d in x_steps:
        from_x[d].wait_recv()
        last_a = last_a + ax_in[d].astype(F32)
    grad_features_ref[0:BS, :] = last_a.T
    grad_bias_ref[...] = w_row[rows_y : rows_y + 1] * scale
    drain()
    for s, _ in ways:
        b_hop[s, half_z].wait_recv()
        last_b = last_b + b_in[way_of[s], half_z - 1].astype(F32)
    grad_features_ref[BS : 2 * BS, :] = last_b.T
    w_copies["bc"][0].wait_recv()
    grad_weights_ref[...] = w_full[...] * scale


def write_kernel(*refs):
    count = (len(refs) - 1) // 2
    sem = refs[-1]
    copies = [pltpu.make_async_copy(refs[i], refs[count + i], sem.at[i]) for i in range(count)]
    for copy in copies:
        copy.start()
    for copy in copies:
        copy.wait()


def mesh_dims(mesh):
    rows, rep = mesh.shape["rows"], mesh.shape["rep"]
    across = 4 if rows >= 32 else 2
    return rows // across, across, rep // 2, 2


def shards(
    dims, features, weights, bias_vector, block_values, block_rows, block_cols, block_live, cotangent
):
    Z, X, Y, K = dims
    nodes, width = features.shape
    hid = weights.shape[1]
    slots = block_values.shape[2]
    half_z = Z // 2
    groups = max(
        group_count(slots, 2 * Y * K, FWD_GROUP, FWD_UNROLL),
        group_count(slots, 2 * Z * X, BWD_GROUP, BWD_PARTS * BWD_UNROLL),
    )
    rows_y = BS // K // Y
    rows_x = -(-(rows_y + 8) // (8 * X)) * 8
    scale = 1.0 / math.sqrt(nodes * Z * X * Y * K)
    vmem = pl.BlockSpec(memory_space=pltpu.VMEM)
    anywhere = pl.BlockSpec(memory_space=pl.ANY)
    hbm = pl.BlockSpec(memory_space=pltpu.HBM)
    block = (BS, BS)
    lists = pl.pallas_call(
        functools.partial(lists_kernel, dims),
        out_shape=jax.ShapeDtypeStruct((16, LIST_WIDTH), jnp.int32),
        in_specs=[hbm, hbm, vmem],
        out_specs=vmem,
        scratch_shapes=[
            pltpu.VMEM(block_rows.shape, jnp.int32),
            pltpu.VMEM(block_cols.shape, jnp.int32),
            pltpu.SemaphoreType.DMA((2,)),
        ],
        name="lists",
    )(block_rows, block_cols, block_live)
    out = pl.pallas_call(
        functools.partial(kernel, dims, scale),
        out_shape=(
            jax.ShapeDtypeStruct((nodes, hid), BF16),
            jax.ShapeDtypeStruct((nodes, width), F32),
            jax.ShapeDtypeStruct((width, hid), F32),
            jax.ShapeDtypeStruct((1, hid), F32),
        ),
        in_specs=[
            hbm,
            hbm,
            hbm,
            hbm,
            anywhere,
            hbm,
        ],
        out_specs=(vmem, vmem, vmem, vmem),
        scratch_shapes=[
            pltpu.SMEM((16, LIST_WIDTH), jnp.int32),
            pltpu.VMEM((slots + 1, *block), BF16),
            pltpu.VMEM((width, hid), BF16),
            pltpu.VMEM((1, hid), F32),
            pltpu.VMEM((nodes, hid), BF16),
            pltpu.VMEM((2 * Z * X, *block), BF16),
            pltpu.VMEM((groups + 1, *block), F32),
            pltpu.VMEM((Y, 2, *block), BF16),
            pltpu.VMEM((Y, 2, *block), BF16),
            pltpu.VMEM((Y, 2, *block), BF16),
            pltpu.VMEM((Y, 2, *block), BF16),
            pltpu.VMEM((2 * Y * K, *block), BF16),
            pltpu.VMEM((2, half_z, X, *block), BF16),
            pltpu.VMEM((2, half_z, X, *block), BF16),
            pltpu.VMEM((X, *block), BF16),
            pltpu.VMEM((X, *block), BF16),
            pltpu.VMEM((X, Z, *block), BF16),
            pltpu.VMEM((X, Z, *block), BF16),
            pltpu.VMEM((2, half_z, *block), BF16),
            pltpu.VMEM((2, half_z, *block), BF16),
            pltpu.VMEM((2, BS // K + 8, hid), F32),
            pltpu.VMEM((BS // K + 8, hid), F32),
            pltpu.VMEM((Y, rows_y + 8, hid), F32),
            pltpu.VMEM((Y, rows_y + 8, hid), F32),
            pltpu.VMEM((rows_x * X, hid), F32),
            pltpu.VMEM((X, rows_x, hid), F32),
            pltpu.VMEM((Z, rows_x, hid), F32),
            pltpu.VMEM((rows_x * X, hid), F32),
            pltpu.VMEM((BS, hid), F32),
            pltpu.SemaphoreType.DMA((SEND_SLOTS,)),
            pltpu.SemaphoreType.DMA((RECV_SLOTS,)),
            pltpu.SemaphoreType.DMA((7,)),
        ],
        compiler_params=pltpu.CompilerParams(
            collective_id=0, has_side_effects=True, vmem_limit_bytes=52 * 1024 * 1024
        ),
        name="layer",
    )(
        features,
        weights,
        bias_vector.reshape(1, hid),
        block_values,
        lists,
        cotangent,
    )
    hidden, grad_features, grad_weights, grad_bias = pl.pallas_call(
        write_kernel,
        out_shape=tuple(jax.ShapeDtypeStruct(a.shape, a.dtype) for a in out),
        in_specs=[vmem] * len(out),
        out_specs=(anywhere,) * len(out),
        scratch_shapes=[pltpu.SemaphoreType.DMA((len(out),))],
        name="write",
    )(*out)
    return hidden, grad_features, grad_weights, grad_bias.reshape(hid)


def solution(mesh):
    in_specs = (
        P(("rows", "rep"), None),
        P(),
        P(),
        P("rows", "rep", None, None, None),
        P("rows", "rep", None),
        P("rows", "rep", None),
        P("rows", "rep"),
        P(("rows", "rep"), None),
    )
    out_specs = (P(("rows", "rep"), None), P(("rows", "rep"), None), P(), P())
    return jax.shard_map(
        functools.partial(shards, mesh_dims(mesh)),
        mesh=mesh,
        in_specs=in_specs,
        out_specs=out_specs,
        check_vma=False,
    )
```

```python
import functools
import math

import jax
import jax.numpy as jnp
from jax import lax
from jax.experimental import pallas as pl
from jax.experimental.pallas import tpu as pltpu
from jax.sharding import PartitionSpec as P

MESH = pl.DeviceIdType.MESH
F32 = jnp.float32
BF16 = jnp.bfloat16
BS = 128
FWD_GROUP = 4
BWD_GROUP = 2
FWD_UNROLL = 23
BWD_UNROLL = 32
BWD_PARTS = 3
SEND_SLOTS = 3
RECV_SLOTS = 99
STAGES = 7
LIST_WIDTH = 384


def group_count(slots, keys, group, unroll):
    groups = (slots + keys * (group - 1)) // group
    return -(-groups // unroll) * unroll


def iota(shape, dim):
    return lax.broadcasted_iota(jnp.int32, shape, dim)


def sorted_lists(key, other, live, keys, group, groups):
    slots = key.shape[1]
    shift = group.bit_length() - 1
    picked = (iota((keys, slots), 0) == key) & live
    one_hot = jnp.where(picked, 1.0, 0.0).astype(F32)
    before = jnp.where(iota((slots, slots), 0) < iota((slots, slots), 1), 1.0, 0.0).astype(BF16)
    place = jnp.dot(one_hot.astype(BF16), before, preferred_element_type=F32)
    count = jnp.sum(one_hot, axis=1, keepdims=True).astype(jnp.int32)
    runs = lax.shift_right_logical(count + (group - 1), shift)
    lower = jnp.where(iota((keys, keys), 1) < iota((keys, keys), 0), 1.0, 0.0).astype(BF16)
    wide_runs = jnp.broadcast_to(runs, (keys, 128)).astype(F32).astype(BF16)
    start = jnp.dot(lower, wide_runs, preferred_element_type=F32)[:, :1]
    target = jnp.sum(one_hot * (start * group + place), axis=0, keepdims=True).astype(jnp.int32)
    target = jnp.where(live, target, -1)
    match = jnp.where(iota((LIST_WIDTH, slots), 0) == target, 1.0, 0.0).astype(BF16)
    number = iota((8, slots), 1)
    line = iota((8, slots), 0)
    facts = jnp.where(
        line == 0,
        lax.shift_right_logical(number, 4),
        jnp.where(line == 1, number & 15, jnp.where(line == 2, jnp.broadcast_to(other, (8, slots)), 1)),
    )
    found = lax.dot_general(
        facts.astype(F32).astype(BF16), match, (((1,), (1,)), ((), ())), preferred_element_type=F32
    ).astype(jnp.int32)
    slot = found[0:1] * 16 + found[1:2] + (1 - found[3:4]) * slots
    partner = found[2:3]
    start_int = start.astype(jnp.int32)
    lane = iota((keys, LIST_WIDTH), 1)
    opens = jnp.sum(jnp.where((start_int == lane) & (count > 0), 1.0, 0.0), axis=0, keepdims=True)
    keep = 1 - opens.astype(jnp.int32)
    final = jnp.where(count > 0, start_int + runs - 1, groups).astype(F32)
    last = jnp.sum(jnp.where(iota((keys, LIST_WIDTH), 0) == lane, final, 0.0), axis=0, keepdims=True)
    out_line = iota((8, LIST_WIDTH), 0)
    return jnp.where(
        out_line == 0,
        slot,
        jnp.where(out_line == 1, partner, jnp.where(out_line == 2, keep, last.astype(jnp.int32))),
    )


def lists_kernel(dims, rows_hbm, cols_hbm, live_ref, lists_ref, rows_ref, cols_ref, sem):
    copies = [
        pltpu.make_async_copy(rows_hbm, rows_ref, sem.at[0]),
        pltpu.make_async_copy(cols_hbm, cols_ref, sem.at[1]),
    ]
    for copy in copies:
        copy.start()
    for copy in copies:
        copy.wait()
    Z, X, Y, K = dims
    slots = rows_ref.shape[2]
    slab_blocks = 2 * Y * K
    col_blocks = 2 * Z * X
    live = iota((1, slots), 1) < live_ref[...]
    fwd_groups = group_count(slots, slab_blocks, FWD_GROUP, FWD_UNROLL)
    bwd_groups = group_count(slots, col_blocks, BWD_GROUP, BWD_PARTS * BWD_UNROLL)
    lists_ref[0:8] = sorted_lists(rows_ref[0], cols_ref[0], live, slab_blocks, FWD_GROUP, fwd_groups)
    lists_ref[8:16] = sorted_lists(cols_ref[0], rows_ref[0], live, col_blocks, BWD_GROUP, bwd_groups)


def kernel(
    dims,
    scale,
    features_hbm,
    weights_hbm,
    bias_hbm,
    values_hbm,
    lists_hbm,
    cotangent_hbm,
    hidden_hbm,
    grad_features_hbm,
    grad_weights_hbm,
    grad_bias_hbm,
    hidden_ref,
    grad_features_ref,
    grad_weights_ref,
    grad_bias_ref,
    lists,
    values,
    weights_ref,
    bias_ref,
    cotangent_ref,
    panel,
    sums,
    core_out,
    core_in,
    y_out,
    y_in,
    agg_t,
    a_out,
    a_in,
    ax_out,
    ax_in,
    bx_out,
    bx_in,
    b_out,
    b_in,
    w_half,
    w_half_in,
    w_y,
    w_y_in,
    w_x,
    w_x_in,
    w_z,
    w_row,
    w_full,
    send_sem,
    recv_sem,
    stage_sem,
    local_sem,
):
    Z, X, Y, K = dims
    slots = values_hbm.shape[2]
    half_z = Z // 2
    half_x = X // 2
    slab_blocks = 2 * Y * K
    col_blocks = 2 * Z * X
    r = lax.axis_index("rows")
    c = lax.axis_index("rep")
    z, x, y, k = lax.div(r, X), lax.rem(r, X), lax.div(c, K), lax.rem(c, K)

    def at_z(step):
        return lax.rem(z + (step + Z), Z)

    def at_x(step):
        return lax.rem(x + (step + X), X)

    def at_y(step):
        return lax.rem(y + (step + Y), Y)

    def device(zz, xx, yy, kk):
        return (zz * X + xx, yy * K + kk)

    other_core = device(z, x, y, 1 - k)
    z_peers = [device(at_z(s), x, y, k) for s in range(1, Z)]
    x_peers = [device(z, at_x(s), y, k) for s in range(1, X)]
    y_peers = [device(z, x, at_y(s), k) for s in range(1, Y)]
    peers = [other_core] + z_peers + x_peers + y_peers

    barrier = pltpu.get_barrier_semaphore()
    for peer in peers:
        pl.semaphore_signal(barrier, inc=1, device_id=peer, device_id_type=MESH)

    load_values = pltpu.make_async_copy(
        values_hbm.at[0, 0], values.at[pl.ds(0, slots)], local_sem.at[0]
    )
    load_own = [
        pltpu.make_async_copy(
            features_hbm.at[pl.ds(i * BS, BS)], panel.at[2 * r + i], local_sem.at[1 + i]
        )
        for i in range(2)
    ]
    for copy in load_own:
        copy.start()
    load_values.start()
    load_layer = [
        pltpu.make_async_copy(weights_hbm, weights_ref, local_sem.at[3]),
        pltpu.make_async_copy(bias_hbm, bias_ref, local_sem.at[4]),
        pltpu.make_async_copy(cotangent_hbm, cotangent_ref, local_sem.at[5]),
    ]
    for copy in load_layer:
        copy.start()
    load_lists = pltpu.make_async_copy(lists_hbm, lists, local_sem.at[6])
    load_lists.start()
    pl.semaphore_wait(barrier, len(peers))
    for copy in load_own:
        copy.wait()

    used = [0]
    bulk = [0, 0]
    staged = []

    def receive_slot():
        used[0] += 1
        return used[0] - 1

    def send(src, dst, to, slot=None, sent=None):
        if sent is None:
            sent = send_sem.at[bulk[0]]
            bulk[1] += math.prod(src.shape)
        copy = pltpu.make_async_remote_copy(
            src_ref=src,
            dst_ref=dst,
            send_sem=sent,
            recv_sem=recv_sem.at[receive_slot() if slot is None else slot],
            device_id=to,
            device_id_type=MESH,
        )
        copy.start()
        return copy

    def whole(ref, slot, sent):
        return pltpu.make_async_remote_copy(
            src_ref=ref,
            dst_ref=ref,
            send_sem=sent,
            recv_sem=recv_sem.at[slot],
            device_id=other_core,
            device_id_type=MESH,
        )

    def wait_group(ref, slot):
        whole(ref, slot, send_sem.at[0]).wait_recv()

    def drain():
        blocks = bulk[1] // (BS * BS)
        assert blocks * BS * BS == bulk[1] and blocks <= panel.shape[0]
        whole(panel.at[pl.ds(0, blocks)], 0, send_sem.at[bulk[0]]).wait_send()
        bulk[0] += 1
        bulk[1] = 0

    def share(piece, to, slot=None):
        return send(piece, piece, to, slot)

    stores = []

    def store(src, dst):
        copy = pltpu.make_async_copy(src, dst, local_sem.at[7 + len(stores)])
        copy.start()
        stores.append(copy)

    def stage(copies, ref):
        slot = receive_slot()
        sent = stage_sem.at[len(staged)]
        for src, dst, to in copies:
            send(src, dst, to, slot, sent)
        staged.append(whole(ref, slot, sent))
        return staged[-1]

    up, down = device(at_z(1), x, y, k), device(at_z(-1), x, y, k)
    ways = ((1, up), (-1, down))
    x_steps = sorted(range(1, X), key=lambda d: -min(d, X - d))

    def shard(zz, xx, part):
        return panel.at[2 * (zz * X + xx) + part]

    halves = {1: pl.ds(0, BS // 2), -1: pl.ds(BS // 2, BS // 2)}
    final = receive_slot()

    a_x = {}
    for d in x_steps:
        a_x[d] = share(shard(z, x, 0), device(z, at_x(d), y, k))
    a_hop = {}
    b_hop = {}
    for s, to in ways:
        a_hop[s, 1, 0] = share(shard(z, x, 0), to)
        b_hop[s, 1] = share(shard(z, x, 1), to)
    for d in x_steps:
        share(shard(z, x, 1), device(z, at_x(d), y, k), final)
    values[slots] = jnp.zeros((BS, BS), BF16)
    fwd_groups = group_count(slots, slab_blocks, FWD_GROUP, FWD_UNROLL)
    bwd_groups = group_count(slots, col_blocks, BWD_GROUP, BWD_PARTS * BWD_UNROLL)
    for d in reversed(x_steps):
        a_x[d].wait_recv()
        for s, to in ways:
            a_hop[s, 1, d] = share(shard(z, at_x(-d), 0), to)
    a_final = 0
    for h in range(1, half_z + 1):
        for s, to in ways:
            b_hop[s, h].wait_recv()
            piece = shard(at_z(-s * h), x, 1)
            if h + 1 < half_z:
                b_hop[s, h + 1] = share(piece, to)
            elif h + 1 == half_z:
                b_hop[s, h + 1] = share(piece.at[halves[s]], to)
            else:
                piece = piece.at[halves[s]]
            for d in x_steps:
                share(piece, device(z, at_x(d), y, k), final)
        for d in range(X):
            for s, to in ways:
                if h < half_z:
                    a_hop[s, h, d].wait_recv()
                    piece = shard(at_z(-s * h), at_x(-d), 0)
                    if h + 1 < half_z:
                        a_hop[s, h + 1, d] = share(piece, to)
                    elif (d < half_x) == (s > 0):
                        share(piece, to, final)
                        a_final += 1
    wait_group(panel.at[pl.ds(0, a_final + Z * (X - 1))], final)
    load_lists.wait()
    load_values.wait()

    zero_block = jnp.zeros((BS, BS), F32)

    def run_groups(line, group, first, groups, unroll, left, right, total):
        def step(base, total):
            for u in range(unroll):
                t = first + base * unroll + u
                at = t * group
                lhs = [left(at + g) for g in range(group)]
                rhs = [right(at + g) for g in range(group)]
                product = jnp.dot(
                    jnp.concatenate(lhs, axis=1),
                    jnp.concatenate(rhs, axis=0),
                    preferred_element_type=F32,
                )
                total = product + total * lists[line + 2, t].astype(F32)
                sums[t] = total
            return total

        assert groups % unroll == 0
        return lax.fori_loop(0, groups // unroll, step, total)

    run_groups(
        0,
        FWD_GROUP,
        0,
        fwd_groups,
        FWD_UNROLL,
        lambda at: values[lists[0, at]],
        lambda at: panel[lists[1, at]],
        zero_block,
    )
    sums[fwd_groups] = zero_block

    drain()

    def row_pair(yy, kk, i):
        return sums[lists[3, 2 * (yy * K + kk) + i]]

    y_steps = sorted(range(1, Y), key=lambda d: -min(d, Y - d))
    from_core = {}
    for d in y_steps + [0]:
        for i in range(2):
            core_out[d, i] = row_pair(at_y(d), 1 - k, i).astype(BF16)
        from_core[d] = send(core_out.at[d], core_in.at[d], other_core)
    from_y = {}
    for d in y_steps:
        from_core[d].wait_recv()
        for i in range(2):
            y_out[d, i] = (row_pair(at_y(d), k, i) + core_in[d, i].astype(F32)).astype(BF16)
        from_y[d] = send(y_out.at[d], y_in.at[d], device(z, x, at_y(d), k))
    from_core[0].wait_recv()
    own = [row_pair(y, k, i) + core_in[0, i].astype(F32) for i in range(2)]
    for d in y_steps:
        from_y[d].wait_recv()
        for i in range(2):
            own[i] = own[i] + y_in[d, i].astype(F32)
    aggregate = jnp.concatenate(own, axis=0).astype(BF16)

    for copy in load_layer:
        copy.wait()
    weights = weights_ref[...]
    preact = jnp.dot(aggregate, weights, preferred_element_type=F32) + bias_ref[...]
    sigma = 1.0 / (1.0 + jnp.exp(-preact))
    deriv = sigma * (1.0 + preact * (1.0 - sigma))
    grad_pre_wide = cotangent_ref[...].astype(F32) * deriv
    grad_pre = grad_pre_wide.astype(BF16)
    grad_t = lax.dot_general(
        weights, grad_pre, (((1,), (1,)), ((), ())), preferred_element_type=F32
    ).astype(BF16)
    agg_t[2 * c] = grad_t[:, 0:BS]
    agg_t[2 * c + 1] = grad_t[:, BS : 2 * BS]

    def slab_pair(yy, kk):
        return agg_t.at[pl.ds(2 * (yy * K + kk), 2)]

    from_y = {}
    for d in y_steps:
        from_y[d] = share(slab_pair(y, k), device(z, x, at_y(d), k))
    core_slot = receive_slot()
    share(slab_pair(y, k), other_core, core_slot)
    hidden_ref[...] = (preact * sigma).astype(BF16)
    store(hidden_ref, hidden_hbm)
    weight_term = lax.dot_general(
        aggregate, grad_pre, (((0,), (0,)), ((), ())), preferred_element_type=F32
    )
    bias_term = jnp.sum(grad_pre.astype(F32), axis=0, keepdims=True)
    grad_weights_ref[...] = weight_term
    rows_core = BS // K
    rows_y = rows_core // Y
    w_tall = rows_y + 8
    rows_x = w_z.shape[1]

    def rows_at(start, size):
        return pl.ds(pl.multiple_of(start, 8), size)

    for i, kk in ((0, 1 - k), (1, k)):
        w_half[i, 0:rows_core] = grad_weights_ref[rows_at(kk * rows_core, rows_core), :]
        w_half[i, rows_core : rows_core + 8] = jnp.broadcast_to(bias_term, (8, bias_term.shape[1]))
    w_core = stage([(w_half.at[0], w_half_in, other_core)], w_half_in)
    for d in reversed(y_steps):
        from_y[d].wait_recv()
        share(slab_pair(at_y(-d), k), other_core, core_slot)
    w_core.wait_recv()
    w_half[1] = w_half[1] + w_half_in[...]
    bias_rows = w_half[1, rows_core : rows_core + 8]
    for d in range(Y):
        w_y[d, 0:rows_y] = w_half[1, rows_at(at_y(d) * rows_y, rows_y), :]
        w_y[d, rows_y:w_tall] = bias_rows
    w_from_y = stage(
        [(w_y.at[d], w_y_in.at[y], device(z, x, at_y(d), k)) for d in y_steps],
        w_y_in.at[pl.ds(0, Y - 1)],
    )
    w_y_in[y] = w_y[0]
    wait_group(agg_t.at[pl.ds(0, 2 * Y)], core_slot)
    drain()

    w_copies = {}

    def stage_x():
        w_from_y.wait_recv()
        total = w_y_in[0]
        for yy in range(1, Y):
            total = total + w_y_in[yy]
        w_x[0:w_tall] = total
        if rows_x * X > w_tall:
            w_x[w_tall : rows_x * X] = jnp.zeros((rows_x * X - w_tall, total.shape[1]), F32)
        w_copies["x"] = stage(
            [
                (w_x.at[rows_at(at_x(d) * rows_x, rows_x)], w_x_in.at[x], device(z, at_x(d), y, k))
                for d in x_steps
            ],
            w_x_in.at[pl.ds(0, X - 1)],
        )
        w_x_in[x] = w_x[rows_at(x * rows_x, rows_x), :]

    def stage_z():
        w_copies["x"].wait_recv()
        total = w_x_in[0]
        for xx in range(1, X):
            total = total + w_x_in[xx]
        w_z[z] = total
        w_copies["z"] = stage(
            [(w_z.at[z], w_z.at[z], peer) for peer in z_peers], w_z.at[pl.ds(0, Z - 1)]
        )

    def stage_back_x():
        w_copies["z"].wait_recv()
        total = w_z[0]
        for zz in range(1, Z):
            total = total + w_z[zz]
        w_row[rows_at(x * rows_x, rows_x), :] = total
        mine = w_row.at[rows_at(x * rows_x, rows_x)]
        w_copies["bx"] = stage(
            [(mine, mine, device(z, at_x(d), y, k)) for d in x_steps],
            w_row.at[pl.ds(0, rows_x * (X - 1))],
        )

    def stage_back_y():
        w_copies["bx"].wait_recv()
        mine = rows_at(k * rows_core + y * rows_y, rows_y)
        w_full[mine, :] = w_row[0:rows_y]
        w_copies["by"] = stage(
            [(w_full.at[mine], w_full.at[mine], device(z, x, at_y(d), k)) for d in y_steps],
            w_full.at[pl.ds(0, rows_y * (Y - 1))],
        )

    def stage_back_core():
        w_copies["by"].wait_recv()
        mine = rows_at(k * rows_core, rows_core)
        w_copies["bc"] = stage([(w_full.at[mine], w_full.at[mine], other_core)], w_full.at[mine])

    stages = [stage_back_y, stage_back_core]

    part_groups = bwd_groups // BWD_PARTS
    running = zero_block
    for part in range(BWD_PARTS):
        running = run_groups(
            8,
            BWD_GROUP,
            part * part_groups,
            part_groups,
            BWD_UNROLL,
            lambda at: agg_t[lists[9, at]],
            lambda at: values[lists[8, at]],
            running,
        )
        if part < 2:
            (stage_x, stage_z)[part]()
    sums[bwd_groups] = zero_block

    def column(zz, xx, part):
        return sums[lists[11, 2 * (zz * X + xx) + part]]

    a_hop = {}
    b_hop = {}
    b_x = {}
    x_slot = receive_slot()

    def send_a(s, to, h, d):
        if h == 1 and (d < half_x) != (s > 0):
            return
        i = 0 if s > 0 else 1
        total = column(at_z(s * (half_z - h + 1)), at_x(d), 0)
        if (s, h - 1, d) in a_hop:
            a_hop[s, h - 1, d].wait_recv()
            total = total + a_in[i, h - 2, d].astype(F32)
        a_out[i, h - 1, d] = total.astype(BF16)
        a_hop[s, h, d] = send(a_out.at[i, h - 1, d], a_in.at[i, h - 1, d], to)

    def send_bx(dz):
        b_x[dz % Z] = receive_slot()
        for i, d in enumerate(x_steps):
            bx_out[dz % Z, i] = column(at_z(dz), at_x(d), 1).astype(BF16)
            send(bx_out.at[dz % Z, i], bx_in.at[dz % Z, i], device(z, at_x(d), y, k), b_x[dz % Z])

    def sum_bx(dz):
        total = column(at_z(dz), x, 1)
        wait_group(bx_in.at[dz % Z, pl.ds(0, X - 1)], b_x[dz % Z])
        for i in range(X - 1):
            total = total + bx_in[dz % Z, i].astype(F32)
        return total

    def send_b(h):
        shared = sum_bx(half_z) if h == 1 else None
        for i, (s, to) in enumerate(ways):
            rows = slice(0, BS // 2) if s > 0 else slice(BS // 2, BS)
            if h == 1:
                b_out[i, 0, rows] = shared[rows].astype(BF16)
                b_hop[s, 1] = send(b_out.at[i, 0, halves[s]], b_in.at[i, 0, halves[s]], to)
                continue
            total = sum_bx(s * (half_z - h + 1))
            b_hop[s, h - 1].wait_recv()
            if h == 2:
                part = total[rows] + b_in[i, 0, rows].astype(F32)
                rest = total[BS // 2 : BS] if s > 0 else total[0 : BS // 2]
                total = jnp.concatenate([part, rest] if s > 0 else [rest, part], axis=0)
            else:
                total = total + b_in[i, h - 2].astype(F32)
            b_out[i, h - 1] = total.astype(BF16)
            b_hop[s, h] = send(b_out.at[i, h - 1], b_in.at[i, h - 1], to)

    for d in range(X):
        for s, to in ways:
            send_a(s, to, 1, d)
    for h in range(half_z, 0, -1):
        send_bx(h)
        if h < half_z:
            send_bx(-h)
        if h == half_z - 1:
            stage_back_x()
    send_bx(0)
    for h in range(2, half_z + 1):
        for d in range(X):
            for s, to in ways:
                send_a(s, to, h, d)
        send_b(h - 1)
        if stages:
            stages.pop(0)()
    last_a = None
    for i, d in enumerate(x_steps + [0]):
        total = column(z, at_x(d), 0)
        for j, (s, _) in enumerate(ways):
            a_hop[s, half_z, d].wait_recv()
            total = total + a_in[j, half_z - 1, d].astype(F32)
        if d:
            ax_out[i] = total.astype(BF16)
            send(ax_out.at[i], ax_in.at[i], device(z, at_x(d), y, k), x_slot)
        else:
            last_a = total
    send_b(half_z)
    while stages:
        stages.pop(0)()
    last_b = sum_bx(0)
    wait_group(ax_in.at[pl.ds(0, X - 1)], x_slot)
    for i in range(X - 1):
        last_a = last_a + ax_in[i].astype(F32)
    grad_features_ref[0:BS, :] = last_a.T
    store(grad_features_ref.at[pl.ds(0, BS)], grad_features_hbm.at[pl.ds(0, BS)])
    grad_bias_ref[...] = w_row[rows_y : rows_y + 1] * scale
    store(grad_bias_ref, grad_bias_hbm)
    w_copies["bc"].wait_recv()
    grad_weights_ref[...] = w_full[...] * scale
    store(grad_weights_ref, grad_weights_hbm)
    drain()
    for i, (s, _) in enumerate(ways):
        b_hop[s, half_z].wait_recv()
        last_b = last_b + b_in[i, half_z - 1].astype(F32)
    grad_features_ref[BS : 2 * BS, :] = last_b.T
    store(grad_features_ref.at[pl.ds(BS, BS)], grad_features_hbm.at[pl.ds(BS, BS)])
    for copy in staged:
        copy.wait_send()
    for copy in stores:
        copy.wait()


def mesh_dims(mesh):
    rows, rep = mesh.shape["rows"], mesh.shape["rep"]
    across = 4 if rows >= 32 else 2
    return rows // across, across, rep // 2, 2


def shards(
    dims, features, weights, bias_vector, block_values, block_rows, block_cols, block_live, cotangent
):
    Z, X, Y, K = dims
    nodes, width = features.shape
    hid = weights.shape[1]
    slots = block_values.shape[2]
    half_z = Z // 2
    groups = max(
        group_count(slots, 2 * Y * K, FWD_GROUP, FWD_UNROLL),
        group_count(slots, 2 * Z * X, BWD_GROUP, BWD_PARTS * BWD_UNROLL),
    )
    rows_y = BS // K // Y
    rows_x = -(-(rows_y + 8) // (8 * X)) * 8
    scale = 1.0 / math.sqrt(nodes * Z * X * Y * K)
    vmem = pl.BlockSpec(memory_space=pltpu.VMEM)
    hbm = pl.BlockSpec(memory_space=pltpu.HBM)
    block = (BS, BS)
    lists = pl.pallas_call(
        functools.partial(lists_kernel, dims),
        out_shape=jax.ShapeDtypeStruct((16, LIST_WIDTH), jnp.int32),
        in_specs=[hbm, hbm, vmem],
        out_specs=vmem,
        scratch_shapes=[
            pltpu.VMEM(block_rows.shape, jnp.int32),
            pltpu.VMEM(block_cols.shape, jnp.int32),
            pltpu.SemaphoreType.DMA((2,)),
        ],
        name="lists",
    )(block_rows, block_cols, block_live)
    out = pl.pallas_call(
        functools.partial(kernel, dims, scale),
        out_shape=(
            jax.ShapeDtypeStruct((nodes, hid), BF16),
            jax.ShapeDtypeStruct((nodes, width), F32),
            jax.ShapeDtypeStruct((width, hid), F32),
            jax.ShapeDtypeStruct((1, hid), F32),
        ),
        in_specs=[
            hbm,
            hbm,
            hbm,
            hbm,
            vmem,
            hbm,
        ],
        out_specs=(hbm, hbm, hbm, hbm),
        scratch_shapes=[
            pltpu.VMEM((nodes, hid), BF16),
            pltpu.VMEM((nodes, width), F32),
            pltpu.VMEM((width, hid), F32),
            pltpu.VMEM((1, hid), F32),
            pltpu.SMEM((16, LIST_WIDTH), jnp.int32),
            pltpu.VMEM((slots + 1, *block), BF16),
            pltpu.VMEM((width, hid), BF16),
            pltpu.VMEM((1, hid), F32),
            pltpu.VMEM((nodes, hid), BF16),
            pltpu.VMEM((2 * Z * X, *block), BF16),
            pltpu.VMEM((groups + 1, *block), F32),
            pltpu.VMEM((Y, 2, *block), BF16),
            pltpu.VMEM((Y, 2, *block), BF16),
            pltpu.VMEM((Y, 2, *block), BF16),
            pltpu.VMEM((Y, 2, *block), BF16),
            pltpu.VMEM((2 * Y * K, *block), BF16),
            pltpu.VMEM((2, half_z, X, *block), BF16),
            pltpu.VMEM((2, half_z, X, *block), BF16),
            pltpu.VMEM((X, *block), BF16),
            pltpu.VMEM((X, *block), BF16),
            pltpu.VMEM((Z, X, *block), BF16),
            pltpu.VMEM((Z, X, *block), BF16),
            pltpu.VMEM((2, half_z, *block), BF16),
            pltpu.VMEM((2, half_z, *block), BF16),
            pltpu.VMEM((2, BS // K + 8, hid), F32),
            pltpu.VMEM((BS // K + 8, hid), F32),
            pltpu.VMEM((Y, rows_y + 8, hid), F32),
            pltpu.VMEM((Y, rows_y + 8, hid), F32),
            pltpu.VMEM((rows_x * X, hid), F32),
            pltpu.VMEM((X, rows_x, hid), F32),
            pltpu.VMEM((Z, rows_x, hid), F32),
            pltpu.VMEM((rows_x * X, hid), F32),
            pltpu.VMEM((BS, hid), F32),
            pltpu.SemaphoreType.DMA((SEND_SLOTS,)),
            pltpu.SemaphoreType.DMA((RECV_SLOTS,)),
            pltpu.SemaphoreType.DMA((STAGES,)),
            pltpu.SemaphoreType.DMA((12,)),
        ],
        compiler_params=pltpu.CompilerParams(
            collective_id=0, has_side_effects=True, vmem_limit_bytes=63 * 1024 * 1024
        ),
        name="layer",
    )(
        features,
        weights,
        bias_vector.reshape(1, hid),
        block_values,
        lists,
        cotangent,
    )
    hidden, grad_features, grad_weights, grad_bias = out
    return hidden, grad_features, grad_weights, grad_bias.reshape(hid)


def solution(mesh):
    in_specs = (
        P(("rows", "rep"), None),
        P(),
        P(),
        P("rows", "rep", None, None, None),
        P("rows", "rep", None),
        P("rows", "rep", None),
        P("rows", "rep"),
        P(("rows", "rep"), None),
    )
    out_specs = (P(("rows", "rep"), None), P(("rows", "rep"), None), P(), P())
    return jax.shard_map(
        functools.partial(shards, mesh_dims(mesh)),
        mesh=mesh,
        in_specs=in_specs,
        out_specs=out_specs,
        check_vma=False,
    )
```

```python
import functools
import math

import jax
import jax.numpy as jnp
from jax import lax
from jax.experimental import pallas as pl
from jax.experimental.pallas import tpu as pltpu
from jax.sharding import PartitionSpec as P

MESH = pl.DeviceIdType.MESH
F32 = jnp.float32
BF16 = jnp.bfloat16
BS = 128
FWD_GROUP = 4
BWD_GROUP = 2
FWD_UNROLL = 23
BWD_UNROLL = 48
BWD_PARTS = 2
SEND_SLOTS = 3
RECV_SLOTS = 99
STAGES = 7
LIST_WIDTH = 384


def group_count(slots, keys, group, unroll):
    groups = (slots + keys * (group - 1)) // group
    return -(-groups // unroll) * unroll


def iota(shape, dim):
    return lax.broadcasted_iota(jnp.int32, shape, dim)


def sorted_lists(key, other, live, keys, group, groups):
    slots = key.shape[1]
    shift = group.bit_length() - 1
    picked = (iota((keys, slots), 0) == key) & live
    one_hot = jnp.where(picked, 1.0, 0.0).astype(F32)
    before = jnp.where(iota((slots, slots), 0) < iota((slots, slots), 1), 1.0, 0.0).astype(BF16)
    place = jnp.dot(one_hot.astype(BF16), before, preferred_element_type=F32)
    count = jnp.sum(one_hot, axis=1, keepdims=True).astype(jnp.int32)
    runs = lax.shift_right_logical(count + (group - 1), shift)
    lower = jnp.where(iota((keys, keys), 1) < iota((keys, keys), 0), 1.0, 0.0).astype(BF16)
    wide_runs = jnp.broadcast_to(runs, (keys, 128)).astype(F32).astype(BF16)
    start = jnp.dot(lower, wide_runs, preferred_element_type=F32)[:, :1]
    target = jnp.sum(one_hot * (start * group + place), axis=0, keepdims=True).astype(jnp.int32)
    target = jnp.where(live, target, -1)
    match = jnp.where(iota((LIST_WIDTH, slots), 0) == target, 1.0, 0.0).astype(BF16)
    number = iota((8, slots), 1)
    line = iota((8, slots), 0)
    facts = jnp.where(
        line == 0,
        lax.shift_right_logical(number, 4),
        jnp.where(line == 1, number & 15, jnp.where(line == 2, jnp.broadcast_to(other, (8, slots)), 1)),
    )
    found = lax.dot_general(
        facts.astype(F32).astype(BF16), match, (((1,), (1,)), ((), ())), preferred_element_type=F32
    ).astype(jnp.int32)
    slot = found[0:1] * 16 + found[1:2] + (1 - found[3:4]) * slots
    partner = found[2:3]
    start_int = start.astype(jnp.int32)
    lane = iota((keys, LIST_WIDTH), 1)
    opens = jnp.sum(jnp.where((start_int == lane) & (count > 0), 1.0, 0.0), axis=0, keepdims=True)
    keep = 1 - opens.astype(jnp.int32)
    final = jnp.where(count > 0, start_int + runs - 1, groups).astype(F32)
    last = jnp.sum(jnp.where(iota((keys, LIST_WIDTH), 0) == lane, final, 0.0), axis=0, keepdims=True)
    out_line = iota((8, LIST_WIDTH), 0)
    return jnp.where(
        out_line == 0,
        slot,
        jnp.where(out_line == 1, partner, jnp.where(out_line == 2, keep, last.astype(jnp.int32))),
    )


def lists_kernel(dims, rows_hbm, cols_hbm, live_ref, lists_ref, rows_ref, cols_ref, sem):
    copies = [
        pltpu.make_async_copy(rows_hbm, rows_ref, sem.at[0]),
        pltpu.make_async_copy(cols_hbm, cols_ref, sem.at[1]),
    ]
    for copy in copies:
        copy.start()
    for copy in copies:
        copy.wait()
    Z, X, Y, K = dims
    slots = rows_ref.shape[2]
    slab_blocks = 2 * Y * K
    col_blocks = 2 * Z * X
    live = iota((1, slots), 1) < live_ref[...]
    fwd_groups = group_count(slots, slab_blocks, FWD_GROUP, FWD_UNROLL)
    bwd_groups = group_count(slots, col_blocks, BWD_GROUP, BWD_PARTS * BWD_UNROLL)
    lists_ref[0:8] = sorted_lists(rows_ref[0], cols_ref[0], live, slab_blocks, FWD_GROUP, fwd_groups)
    lists_ref[8:16] = sorted_lists(cols_ref[0], rows_ref[0], live, col_blocks, BWD_GROUP, bwd_groups)


def kernel(
    dims,
    scale,
    features_hbm,
    weights_hbm,
    bias_hbm,
    values_hbm,
    lists_hbm,
    cotangent_hbm,
    hidden_ref,
    grad_features_ref,
    grad_weights_ref,
    grad_bias_ref,
    lists,
    values,
    weights_ref,
    bias_ref,
    cotangent_ref,
    panel,
    sums,
    core_out,
    core_in,
    y_out,
    y_in,
    agg_t,
    a_out,
    a_in,
    ax_out,
    ax_in,
    bx_out,
    bx_in,
    b_out,
    b_in,
    w_half,
    w_half_in,
    w_y,
    w_y_in,
    w_x,
    w_x_in,
    w_z,
    w_row,
    w_full,
    send_sem,
    recv_sem,
    stage_sem,
    local_sem,
):
    Z, X, Y, K = dims
    slots = values_hbm.shape[2]
    half_z = Z // 2
    half_x = X // 2
    slab_blocks = 2 * Y * K
    col_blocks = 2 * Z * X
    r = lax.axis_index("rows")
    c = lax.axis_index("rep")
    z, x, y, k = lax.div(r, X), lax.rem(r, X), lax.div(c, K), lax.rem(c, K)

    def at_z(step):
        return lax.rem(z + (step + Z), Z)

    def at_x(step):
        return lax.rem(x + (step + X), X)

    def at_y(step):
        return lax.rem(y + (step + Y), Y)

    def device(zz, xx, yy, kk):
        return (zz * X + xx, yy * K + kk)

    other_core = device(z, x, y, 1 - k)
    z_peers = [device(at_z(s), x, y, k) for s in range(1, Z)]
    x_peers = [device(z, at_x(s), y, k) for s in range(1, X)]
    y_peers = [device(z, x, at_y(s), k) for s in range(1, Y)]
    peers = [other_core] + z_peers + x_peers + y_peers

    barrier = pltpu.get_barrier_semaphore()
    for peer in peers:
        pl.semaphore_signal(barrier, inc=1, device_id=peer, device_id_type=MESH)

    load_values = pltpu.make_async_copy(
        values_hbm.at[0, 0], values.at[pl.ds(0, slots)], local_sem.at[0]
    )
    load_own = [
        pltpu.make_async_copy(
            features_hbm.at[pl.ds(i * BS, BS)], panel.at[2 * r + i], local_sem.at[1 + i]
        )
        for i in range(2)
    ]
    for copy in load_own:
        copy.start()
    load_values.start()
    load_layer = [
        pltpu.make_async_copy(weights_hbm, weights_ref, local_sem.at[3]),
        pltpu.make_async_copy(bias_hbm, bias_ref, local_sem.at[4]),
        pltpu.make_async_copy(cotangent_hbm, cotangent_ref, local_sem.at[5]),
    ]
    for copy in load_layer:
        copy.start()
    load_lists = pltpu.make_async_copy(lists_hbm, lists, local_sem.at[6])
    load_lists.start()
    pl.semaphore_wait(barrier, len(peers))
    for copy in load_own:
        copy.wait()

    used = [0]
    bulk = [0, 0]
    staged = []

    def receive_slot():
        used[0] += 1
        return used[0] - 1

    def send(src, dst, to, slot=None, sent=None):
        if sent is None:
            sent = send_sem.at[bulk[0]]
            bulk[1] += math.prod(src.shape)
        copy = pltpu.make_async_remote_copy(
            src_ref=src,
            dst_ref=dst,
            send_sem=sent,
            recv_sem=recv_sem.at[receive_slot() if slot is None else slot],
            device_id=to,
            device_id_type=MESH,
        )
        copy.start()
        return copy

    def whole(ref, slot, sent):
        return pltpu.make_async_remote_copy(
            src_ref=ref,
            dst_ref=ref,
            send_sem=sent,
            recv_sem=recv_sem.at[slot],
            device_id=other_core,
            device_id_type=MESH,
        )

    def wait_group(ref, slot):
        whole(ref, slot, send_sem.at[0]).wait_recv()

    def drain():
        blocks = bulk[1] // (BS * BS)
        assert blocks * BS * BS == bulk[1] and blocks <= panel.shape[0]
        whole(panel.at[pl.ds(0, blocks)], 0, send_sem.at[bulk[0]]).wait_send()
        bulk[0] += 1
        bulk[1] = 0

    def share(piece, to, slot=None):
        return send(piece, piece, to, slot)

    def stage(copies, ref):
        slot = receive_slot()
        sent = stage_sem.at[len(staged)]
        for src, dst, to in copies:
            send(src, dst, to, slot, sent)
        staged.append(whole(ref, slot, sent))
        return staged[-1]

    up, down = device(at_z(1), x, y, k), device(at_z(-1), x, y, k)
    ways = ((1, up), (-1, down))
    x_steps = sorted(range(1, X), key=lambda d: -min(d, X - d))

    def shard(zz, xx, part):
        return panel.at[2 * (zz * X + xx) + part]

    halves = {1: pl.ds(0, BS // 2), -1: pl.ds(BS // 2, BS // 2)}
    final = receive_slot()

    a_x = {}
    for d in x_steps:
        a_x[d] = share(shard(z, x, 0), device(z, at_x(d), y, k))
    a_hop = {}
    b_hop = {}
    for s, to in ways:
        a_hop[s, 1, 0] = share(shard(z, x, 0), to)
        b_hop[s, 1] = share(shard(z, x, 1), to)
    for d in x_steps:
        share(shard(z, x, 1), device(z, at_x(d), y, k), final)
    values[slots] = jnp.zeros((BS, BS), BF16)
    fwd_groups = group_count(slots, slab_blocks, FWD_GROUP, FWD_UNROLL)
    bwd_groups = group_count(slots, col_blocks, BWD_GROUP, BWD_PARTS * BWD_UNROLL)
    for d in reversed(x_steps):
        a_x[d].wait_recv()
        for s, to in ways:
            a_hop[s, 1, d] = share(shard(z, at_x(-d), 0), to)
    a_final = 0
    for h in range(1, half_z + 1):
        for s, to in ways:
            b_hop[s, h].wait_recv()
            piece = shard(at_z(-s * h), x, 1)
            if h + 1 < half_z:
                b_hop[s, h + 1] = share(piece, to)
            elif h + 1 == half_z:
                b_hop[s, h + 1] = share(piece.at[halves[s]], to)
            else:
                piece = piece.at[halves[s]]
            for d in x_steps:
                share(piece, device(z, at_x(d), y, k), final)
        for d in range(X):
            for s, to in ways:
                if h < half_z:
                    a_hop[s, h, d].wait_recv()
                    piece = shard(at_z(-s * h), at_x(-d), 0)
                    if h + 1 < half_z:
                        a_hop[s, h + 1, d] = share(piece, to)
                    elif (d < half_x) == (s > 0):
                        share(piece, to, final)
                        a_final += 1
    wait_group(panel.at[pl.ds(0, a_final + Z * (X - 1))], final)
    load_lists.wait()
    load_values.wait()

    zero_block = jnp.zeros((BS, BS), F32)

    def run_groups(line, group, first, groups, unroll, left, right, total):
        def step(base, total):
            for u in range(unroll):
                t = first + base * unroll + u
                at = t * group
                lhs = [left(at + g) for g in range(group)]
                rhs = [right(at + g) for g in range(group)]
                product = jnp.dot(
                    jnp.concatenate(lhs, axis=1),
                    jnp.concatenate(rhs, axis=0),
                    preferred_element_type=F32,
                )
                total = product + total * lists[line + 2, t].astype(F32)
                sums[t] = total
            return total

        assert groups % unroll == 0
        return lax.fori_loop(0, groups // unroll, step, total)

    run_groups(
        0,
        FWD_GROUP,
        0,
        fwd_groups,
        FWD_UNROLL,
        lambda at: values[lists[0, at]],
        lambda at: panel[lists[1, at]],
        zero_block,
    )
    sums[fwd_groups] = zero_block

    drain()

    def row_pair(yy, kk, i):
        return sums[lists[3, 2 * (yy * K + kk) + i]]

    y_steps = sorted(range(1, Y), key=lambda d: -min(d, Y - d))
    from_core = {}
    for d in y_steps + [0]:
        for i in range(2):
            core_out[d, i] = row_pair(at_y(d), 1 - k, i).astype(BF16)
        from_core[d] = send(core_out.at[d], core_in.at[d], other_core)
    from_y = {}
    for d in y_steps:
        from_core[d].wait_recv()
        for i in range(2):
            y_out[d, i] = (row_pair(at_y(d), k, i) + core_in[d, i].astype(F32)).astype(BF16)
        from_y[d] = send(y_out.at[d], y_in.at[d], device(z, x, at_y(d), k))
    from_core[0].wait_recv()
    own = [row_pair(y, k, i) + core_in[0, i].astype(F32) for i in range(2)]
    for d in y_steps:
        from_y[d].wait_recv()
        for i in range(2):
            own[i] = own[i] + y_in[d, i].astype(F32)
    aggregate = jnp.concatenate(own, axis=0).astype(BF16)

    for copy in load_layer:
        copy.wait()
    weights = weights_ref[...]
    preact = jnp.dot(aggregate, weights, preferred_element_type=F32) + bias_ref[...]
    sigma = 1.0 / (1.0 + jnp.exp(-preact))
    deriv = sigma * (1.0 + preact * (1.0 - sigma))
    grad_pre_wide = cotangent_ref[...].astype(F32) * deriv
    grad_pre = grad_pre_wide.astype(BF16)
    grad_t = lax.dot_general(
        weights, grad_pre, (((1,), (1,)), ((), ())), preferred_element_type=F32
    ).astype(BF16)
    agg_t[2 * c] = grad_t[:, 0:BS]
    agg_t[2 * c + 1] = grad_t[:, BS : 2 * BS]

    def slab_pair(yy, kk):
        return agg_t.at[pl.ds(2 * (yy * K + kk), 2)]

    from_y = {}
    for d in y_steps:
        from_y[d] = share(slab_pair(y, k), device(z, x, at_y(d), k))
    core_slot = receive_slot()
    share(slab_pair(y, k), other_core, core_slot)
    hidden_ref[...] = (preact * sigma).astype(BF16)
    weight_term = lax.dot_general(
        aggregate, grad_pre, (((0,), (0,)), ((), ())), preferred_element_type=F32
    )
    bias_term = jnp.sum(grad_pre.astype(F32), axis=0, keepdims=True)
    grad_weights_ref[...] = weight_term
    rows_core = BS // K
    rows_y = rows_core // Y
    w_tall = rows_y + 8
    rows_x = w_z.shape[1]

    def rows_at(start, size):
        return pl.ds(pl.multiple_of(start, 8), size)

    for i, kk in ((0, 1 - k), (1, k)):
        w_half[i, 0:rows_core] = grad_weights_ref[rows_at(kk * rows_core, rows_core), :]
        w_half[i, rows_core : rows_core + 8] = jnp.broadcast_to(bias_term, (8, bias_term.shape[1]))
    w_core = stage([(w_half.at[0], w_half_in, other_core)], w_half_in)
    for d in reversed(y_steps):
        from_y[d].wait_recv()
        share(slab_pair(at_y(-d), k), other_core, core_slot)
    w_core.wait_recv()
    w_half[1] = w_half[1] + w_half_in[...]
    bias_rows = w_half[1, rows_core : rows_core + 8]
    for d in range(Y):
        w_y[d, 0:rows_y] = w_half[1, rows_at(at_y(d) * rows_y, rows_y), :]
        w_y[d, rows_y:w_tall] = bias_rows
    w_from_y = stage(
        [(w_y.at[d], w_y_in.at[y], device(z, x, at_y(d), k)) for d in y_steps],
        w_y_in.at[pl.ds(0, Y - 1)],
    )
    w_y_in[y] = w_y[0]
    wait_group(agg_t.at[pl.ds(0, 2 * Y)], core_slot)
    drain()

    w_copies = {}

    def stage_x():
        w_from_y.wait_recv()
        total = w_y_in[0]
        for yy in range(1, Y):
            total = total + w_y_in[yy]
        w_x[0:w_tall] = total
        if rows_x * X > w_tall:
            w_x[w_tall : rows_x * X] = jnp.zeros((rows_x * X - w_tall, total.shape[1]), F32)
        w_copies["x"] = stage(
            [
                (w_x.at[rows_at(at_x(d) * rows_x, rows_x)], w_x_in.at[x], device(z, at_x(d), y, k))
                for d in x_steps
            ],
            w_x_in.at[pl.ds(0, X - 1)],
        )
        w_x_in[x] = w_x[rows_at(x * rows_x, rows_x), :]

    def stage_z():
        w_copies["x"].wait_recv()
        total = w_x_in[0]
        for xx in range(1, X):
            total = total + w_x_in[xx]
        w_z[z] = total
        w_copies["z"] = stage(
            [(w_z.at[z], w_z.at[z], peer) for peer in z_peers], w_z.at[pl.ds(0, Z - 1)]
        )

    def stage_back_x():
        w_copies["z"].wait_recv()
        total = w_z[0]
        for zz in range(1, Z):
            total = total + w_z[zz]
        w_row[rows_at(x * rows_x, rows_x), :] = total
        mine = w_row.at[rows_at(x * rows_x, rows_x)]
        w_copies["bx"] = stage(
            [(mine, mine, device(z, at_x(d), y, k)) for d in x_steps],
            w_row.at[pl.ds(0, rows_x * (X - 1))],
        )

    def stage_back_y():
        w_copies["bx"].wait_recv()
        mine = rows_at(k * rows_core + y * rows_y, rows_y)
        w_full[mine, :] = w_row[0:rows_y]
        w_copies["by"] = stage(
            [(w_full.at[mine], w_full.at[mine], device(z, x, at_y(d), k)) for d in y_steps],
            w_full.at[pl.ds(0, rows_y * (Y - 1))],
        )

    def stage_back_core():
        w_copies["by"].wait_recv()
        mine = rows_at(k * rows_core, rows_core)
        w_copies["bc"] = stage([(w_full.at[mine], w_full.at[mine], other_core)], w_full.at[mine])

    stages = [stage_back_x, stage_back_y, stage_back_core]

    part_groups = bwd_groups // BWD_PARTS
    running = zero_block
    for part in range(BWD_PARTS):
        running = run_groups(
            8,
            BWD_GROUP,
            part * part_groups,
            part_groups,
            BWD_UNROLL,
            lambda at: agg_t[lists[9, at]],
            lambda at: values[lists[8, at]],
            running,
        )
        (stage_x, stage_z)[part]()
    sums[bwd_groups] = zero_block

    def column(zz, xx, part):
        return sums[lists[11, 2 * (zz * X + xx) + part]]

    a_hop = {}
    b_hop = {}
    b_x = {}
    x_slot = receive_slot()

    def send_a(s, to, h, d):
        if h == 1 and (d < half_x) != (s > 0):
            return
        i = 0 if s > 0 else 1
        total = column(at_z(s * (half_z - h + 1)), at_x(d), 0)
        if (s, h - 1, d) in a_hop:
            a_hop[s, h - 1, d].wait_recv()
            total = total + a_in[i, h - 2, d].astype(F32)
        a_out[i, h - 1, d] = total.astype(BF16)
        a_hop[s, h, d] = send(a_out.at[i, h - 1, d], a_in.at[i, h - 1, d], to)

    def send_bx(dz):
        b_x[dz % Z] = receive_slot()
        for i, d in enumerate(x_steps):
            bx_out[dz % Z, i] = column(at_z(dz), at_x(d), 1).astype(BF16)
            send(bx_out.at[dz % Z, i], bx_in.at[dz % Z, i], device(z, at_x(d), y, k), b_x[dz % Z])

    def sum_bx(dz):
        total = column(at_z(dz), x, 1)
        wait_group(bx_in.at[dz % Z, pl.ds(0, X - 1)], b_x[dz % Z])
        for i in range(X - 1):
            total = total + bx_in[dz % Z, i].astype(F32)
        return total

    def send_b(h):
        shared = sum_bx(half_z) if h == 1 else None
        for i, (s, to) in enumerate(ways):
            rows = slice(0, BS // 2) if s > 0 else slice(BS // 2, BS)
            if h == 1:
                b_out[i, 0, rows] = shared[rows].astype(BF16)
                b_hop[s, 1] = send(b_out.at[i, 0, halves[s]], b_in.at[i, 0, halves[s]], to)
                continue
            total = sum_bx(s * (half_z - h + 1))
            b_hop[s, h - 1].wait_recv()
            if h == 2:
                part = total[rows] + b_in[i, 0, rows].astype(F32)
                rest = total[BS // 2 : BS] if s > 0 else total[0 : BS // 2]
                total = jnp.concatenate([part, rest] if s > 0 else [rest, part], axis=0)
            else:
                total = total + b_in[i, h - 2].astype(F32)
            b_out[i, h - 1] = total.astype(BF16)
            b_hop[s, h] = send(b_out.at[i, h - 1], b_in.at[i, h - 1], to)

    for d in range(X):
        for s, to in ways:
            send_a(s, to, 1, d)
    send_bx(half_z)
    for h in range(half_z - 1, 1, -1):
        send_bx(h)
        send_bx(-h)
    for h in range(2, half_z + 1):
        for d in range(X):
            for s, to in ways:
                send_a(s, to, h, d)
        send_b(h - 1)
        if stages:
            stages.pop(0)()
        if h == 2:
            for near in (1, -1, 0):
                send_bx(near)
    last_a = None
    for i, d in enumerate(x_steps + [0]):
        total = column(z, at_x(d), 0)
        for j, (s, _) in enumerate(ways):
            a_hop[s, half_z, d].wait_recv()
            total = total + a_in[j, half_z - 1, d].astype(F32)
        if d:
            ax_out[i] = total.astype(BF16)
            send(ax_out.at[i], ax_in.at[i], device(z, at_x(d), y, k), x_slot)
        else:
            last_a = total
    send_b(half_z)
    while stages:
        stages.pop(0)()
    last_b = sum_bx(0)
    wait_group(ax_in.at[pl.ds(0, X - 1)], x_slot)
    for i in range(X - 1):
        last_a = last_a + ax_in[i].astype(F32)
    grad_features_ref[0:BS, :] = last_a.T
    grad_bias_ref[...] = w_row[rows_y : rows_y + 1] * scale
    w_copies["bc"].wait_recv()
    grad_weights_ref[...] = w_full[...] * scale
    drain()
    for i, (s, _) in enumerate(ways):
        b_hop[s, half_z].wait_recv()
        last_b = last_b + b_in[i, half_z - 1].astype(F32)
    grad_features_ref[BS : 2 * BS, :] = last_b.T
    for copy in staged:
        copy.wait_send()


def mesh_dims(mesh):
    rows, rep = mesh.shape["rows"], mesh.shape["rep"]
    across = 4 if rows >= 32 else 2
    return rows // across, across, rep // 2, 2


def shards(
    dims, features, weights, bias_vector, block_values, block_rows, block_cols, block_live, cotangent
):
    Z, X, Y, K = dims
    nodes, width = features.shape
    hid = weights.shape[1]
    slots = block_values.shape[2]
    half_z = Z // 2
    groups = max(
        group_count(slots, 2 * Y * K, FWD_GROUP, FWD_UNROLL),
        group_count(slots, 2 * Z * X, BWD_GROUP, BWD_PARTS * BWD_UNROLL),
    )
    rows_y = BS // K // Y
    rows_x = -(-(rows_y + 8) // (8 * X)) * 8
    scale = 1.0 / math.sqrt(nodes * Z * X * Y * K)
    vmem = pl.BlockSpec(memory_space=pltpu.VMEM)
    hbm = pl.BlockSpec(memory_space=pltpu.HBM)
    block = (BS, BS)
    lists = pl.pallas_call(
        functools.partial(lists_kernel, dims),
        out_shape=jax.ShapeDtypeStruct((16, LIST_WIDTH), jnp.int32),
        in_specs=[hbm, hbm, vmem],
        out_specs=vmem,
        scratch_shapes=[
            pltpu.VMEM(block_rows.shape, jnp.int32),
            pltpu.VMEM(block_cols.shape, jnp.int32),
            pltpu.SemaphoreType.DMA((2,)),
        ],
        name="lists",
    )(block_rows, block_cols, block_live)
    out = pl.pallas_call(
        functools.partial(kernel, dims, scale),
        out_shape=(
            pltpu.VMEM((nodes, hid), BF16),
            pltpu.VMEM((nodes, width), F32),
            pltpu.VMEM((width, hid), F32),
            pltpu.VMEM((1, hid), F32),
        ),
        in_specs=[
            hbm,
            hbm,
            hbm,
            hbm,
            vmem,
            hbm,
        ],
        out_specs=(vmem, vmem, vmem, vmem),
        scratch_shapes=[
            pltpu.SMEM((16, LIST_WIDTH), jnp.int32),
            pltpu.VMEM((slots + 1, *block), BF16),
            pltpu.VMEM((width, hid), BF16),
            pltpu.VMEM((1, hid), F32),
            pltpu.VMEM((nodes, hid), BF16),
            pltpu.VMEM((2 * Z * X, *block), BF16),
            pltpu.VMEM((groups + 1, *block), F32),
            pltpu.VMEM((Y, 2, *block), BF16),
            pltpu.VMEM((Y, 2, *block), BF16),
            pltpu.VMEM((Y, 2, *block), BF16),
            pltpu.VMEM((Y, 2, *block), BF16),
            pltpu.VMEM((2 * Y * K, *block), BF16),
            pltpu.VMEM((2, half_z, X, *block), BF16),
            pltpu.VMEM((2, half_z, X, *block), BF16),
            pltpu.VMEM((X, *block), BF16),
            pltpu.VMEM((X, *block), BF16),
            pltpu.VMEM((Z, X, *block), BF16),
            pltpu.VMEM((Z, X, *block), BF16),
            pltpu.VMEM((2, half_z, *block), BF16),
            pltpu.VMEM((2, half_z, *block), BF16),
            pltpu.VMEM((2, BS // K + 8, hid), F32),
            pltpu.VMEM((BS // K + 8, hid), F32),
            pltpu.VMEM((Y, rows_y + 8, hid), F32),
            pltpu.VMEM((Y, rows_y + 8, hid), F32),
            pltpu.VMEM((rows_x * X, hid), F32),
            pltpu.VMEM((X, rows_x, hid), F32),
            pltpu.VMEM((Z, rows_x, hid), F32),
            pltpu.VMEM((rows_x * X, hid), F32),
            pltpu.VMEM((BS, hid), F32),
            pltpu.SemaphoreType.DMA((SEND_SLOTS,)),
            pltpu.SemaphoreType.DMA((RECV_SLOTS,)),
            pltpu.SemaphoreType.DMA((STAGES,)),
            pltpu.SemaphoreType.DMA((7,)),
        ],
        compiler_params=pltpu.CompilerParams(
            collective_id=0, has_side_effects=True, vmem_limit_bytes=63 * 1024 * 1024
        ),
        name="layer",
    )(
        features,
        weights,
        bias_vector.reshape(1, hid),
        block_values,
        lists,
        cotangent,
    )
    hidden, grad_features, grad_weights, grad_bias = out
    return hidden, grad_features, grad_weights, grad_bias.reshape(hid)


def solution(mesh):
    in_specs = (
        P(("rows", "rep"), None),
        P(),
        P(),
        P("rows", "rep", None, None, None),
        P("rows", "rep", None),
        P("rows", "rep", None),
        P("rows", "rep"),
        P(("rows", "rep"), None),
    )
    out_specs = (P(("rows", "rep"), None), P(("rows", "rep"), None), P(), P())
    return jax.shard_map(
        functools.partial(shards, mesh_dims(mesh)),
        mesh=mesh,
        in_specs=in_specs,
        out_specs=out_specs,
        check_vma=False,
    )
```

```python
import functools
import math

import jax
import jax.numpy as jnp
from jax import lax
from jax.experimental import pallas as pl
from jax.experimental.pallas import tpu as pltpu
from jax.sharding import PartitionSpec as P

MESH = pl.DeviceIdType.MESH
F32 = jnp.float32
BF16 = jnp.bfloat16
BS = 128
FWD_GROUP = 4
BWD_GROUP = 2
FWD_UNROLL = 46
BWD_UNROLL = 48
BWD_PARTS = 2
SEND_SLOTS = 3
RECV_SLOTS = 99
STAGES = 7
LIST_WIDTH = 384


def group_count(slots, keys, group, unroll):
    groups = (slots + keys * (group - 1)) // group
    return -(-groups // unroll) * unroll


def iota(shape, dim):
    return lax.broadcasted_iota(jnp.int32, shape, dim)


def sorted_lists(key, other, live, keys, partners, group, groups):
    slots = key.shape[1]
    shift = group.bit_length() - 1
    picked = (iota((keys, slots), 0) == key) & live
    one_hot = jnp.where(picked, 1.0, 0.0).astype(F32)
    before = jnp.where(iota((slots, slots), 0) < iota((slots, slots), 1), 1.0, 0.0).astype(BF16)
    place = jnp.dot(one_hot.astype(BF16), before, preferred_element_type=F32)
    count = jnp.sum(one_hot, axis=1, keepdims=True).astype(jnp.int32)
    runs = lax.shift_right_logical(count + (group - 1), shift)
    lower = jnp.where(iota((keys, keys), 1) < iota((keys, keys), 0), 1.0, 0.0).astype(BF16)
    wide_runs = jnp.broadcast_to(runs, (keys, 128)).astype(F32).astype(BF16)
    start = jnp.dot(lower, wide_runs, preferred_element_type=F32)[:, :1]
    target = jnp.sum(one_hot * (start * group + place), axis=0, keepdims=True).astype(jnp.int32)
    target = jnp.where(live, target, -1)
    match = jnp.where(iota((LIST_WIDTH, slots), 0) == target, 1.0, 0.0).astype(BF16)
    number = iota((8, slots), 1)
    line = iota((8, slots), 0)
    facts = jnp.where(
        line == 0,
        lax.shift_right_logical(number, 4),
        jnp.where(line == 1, number & 15, jnp.where(line == 2, jnp.broadcast_to(other, (8, slots)), 1)),
    )
    found = lax.dot_general(
        facts.astype(F32).astype(BF16), match, (((1,), (1,)), ((), ())), preferred_element_type=F32
    ).astype(jnp.int32)
    slot = found[0:1] * 16 + found[1:2] + (1 - found[3:4]) * slots
    partner = found[2:3]
    start_int = start.astype(jnp.int32)
    lane = iota((keys, LIST_WIDTH), 1)
    opens = jnp.sum(jnp.where((start_int == lane) & (count > 0), 1.0, 0.0), axis=0, keepdims=True)
    keep = 1 - opens.astype(jnp.int32)
    final = jnp.where(count > 0, start_int + runs - 1, groups).astype(F32)
    last = jnp.sum(jnp.where(iota((keys, LIST_WIDTH), 0) == lane, final, 0.0), axis=0, keepdims=True)
    out_line = iota((8, LIST_WIDTH), 0)
    slot = jnp.clip(slot, 0, slots)
    partner = jnp.clip(partner, 0, partners - 1)
    keep = jnp.clip(keep, 0, 1)
    last = jnp.clip(last.astype(jnp.int32), 0, groups)
    return jnp.where(
        out_line == 0,
        slot,
        jnp.where(out_line == 1, partner, jnp.where(out_line == 2, keep, last)),
    )


def kernel(
    dims,
    scale,
    features_hbm,
    weights_hbm,
    bias_hbm,
    values_hbm,
    rows_hbm,
    cols_hbm,
    live_ref,
    cotangent_hbm,
    hidden_ref,
    grad_features_ref,
    grad_weights_ref,
    grad_bias_ref,
    fwd_list,
    bwd_list,
    lists_vmem,
    rows_ref,
    cols_ref,
    values,
    weights_ref,
    bias_ref,
    cotangent_ref,
    panel,
    sums,
    core_out,
    core_in,
    y_out,
    y_in,
    agg_t,
    a_out,
    a_in,
    ax_out,
    ax_in,
    bx_out,
    bx_in,
    b_out,
    b_in,
    w_half,
    w_half_in,
    w_y,
    w_y_in,
    w_x,
    w_x_in,
    w_z,
    w_row,
    w_full,
    send_sem,
    recv_sem,
    stage_sem,
    local_sem,
):
    Z, X, Y, K = dims
    slots = values_hbm.shape[2]
    half_z = Z // 2
    half_x = X // 2
    slab_blocks = 2 * Y * K
    col_blocks = 2 * Z * X
    r = lax.axis_index("rows")
    c = lax.axis_index("rep")
    z, x, y, k = lax.div(r, X), lax.rem(r, X), lax.div(c, K), lax.rem(c, K)

    def at_z(step):
        return lax.rem(z + (step + Z), Z)

    def at_x(step):
        return lax.rem(x + (step + X), X)

    def at_y(step):
        return lax.rem(y + (step + Y), Y)

    def device(zz, xx, yy, kk):
        return (zz * X + xx, yy * K + kk)

    other_core = device(z, x, y, 1 - k)
    z_peers = [device(at_z(s), x, y, k) for s in range(1, Z)]
    x_peers = [device(z, at_x(s), y, k) for s in range(1, X)]
    y_peers = [device(z, x, at_y(s), k) for s in range(1, Y)]
    peers = [other_core] + z_peers + x_peers + y_peers

    barrier = pltpu.get_barrier_semaphore()
    for peer in peers:
        pl.semaphore_signal(barrier, inc=1, device_id=peer, device_id_type=MESH)

    load_values = pltpu.make_async_copy(
        values_hbm.at[0, 0], values.at[pl.ds(0, slots)], local_sem.at[0]
    )
    load_own = [
        pltpu.make_async_copy(
            features_hbm.at[pl.ds(i * BS, BS)], panel.at[2 * r + i], local_sem.at[1 + i]
        )
        for i in range(2)
    ]
    for copy in load_own:
        copy.start()
    load_values.start()
    load_layer = [
        pltpu.make_async_copy(weights_hbm, weights_ref, local_sem.at[3]),
        pltpu.make_async_copy(bias_hbm, bias_ref, local_sem.at[4]),
        pltpu.make_async_copy(cotangent_hbm, cotangent_ref, local_sem.at[5]),
    ]
    for copy in load_layer:
        copy.start()
    load_index = [
        pltpu.make_async_copy(rows_hbm, rows_ref, local_sem.at[6]),
        pltpu.make_async_copy(cols_hbm, cols_ref, local_sem.at[7]),
    ]
    for copy in load_index:
        copy.start()
    pl.semaphore_wait(barrier, len(peers))
    for copy in load_own:
        copy.wait()

    used = [0]
    bulk = [0, 0]
    staged = []

    def receive_slot():
        used[0] += 1
        return used[0] - 1

    def send(src, dst, to, slot=None, sent=None):
        if sent is None:
            sent = send_sem.at[bulk[0]]
            bulk[1] += math.prod(src.shape)
        copy = pltpu.make_async_remote_copy(
            src_ref=src,
            dst_ref=dst,
            send_sem=sent,
            recv_sem=recv_sem.at[receive_slot() if slot is None else slot],
            device_id=to,
            device_id_type=MESH,
        )
        copy.start()
        return copy

    def whole(ref, slot, sent):
        return pltpu.make_async_remote_copy(
            src_ref=ref,
            dst_ref=ref,
            send_sem=sent,
            recv_sem=recv_sem.at[slot],
            device_id=other_core,
            device_id_type=MESH,
        )

    def wait_group(ref, slot):
        whole(ref, slot, send_sem.at[0]).wait_recv()

    def drain():
        blocks = bulk[1] // (BS * BS)
        assert blocks * BS * BS == bulk[1] and blocks <= panel.shape[0]
        whole(panel.at[pl.ds(0, blocks)], 0, send_sem.at[bulk[0]]).wait_send()
        bulk[0] += 1
        bulk[1] = 0

    def share(piece, to, slot=None):
        return send(piece, piece, to, slot)

    def stage(copies, ref):
        slot = receive_slot()
        sent = stage_sem.at[len(staged)]
        for src, dst, to in copies:
            send(src, dst, to, slot, sent)
        staged.append(whole(ref, slot, sent))
        return staged[-1]

    up, down = device(at_z(1), x, y, k), device(at_z(-1), x, y, k)
    ways = ((1, up), (-1, down))
    x_steps = sorted(range(1, X), key=lambda d: -min(d, X - d))

    def shard(zz, xx, part):
        return panel.at[2 * (zz * X + xx) + part]

    halves = {1: pl.ds(0, BS // 2), -1: pl.ds(BS // 2, BS // 2)}
    final = receive_slot()

    a_x = {}
    for d in x_steps:
        a_x[d] = share(shard(z, x, 0), device(z, at_x(d), y, k))
    a_hop = {}
    b_hop = {}
    for s, to in ways:
        a_hop[s, 1, 0] = share(shard(z, x, 0), to)
        b_hop[s, 1] = share(shard(z, x, 1), to)
    for d in x_steps:
        share(shard(z, x, 1), device(z, at_x(d), y, k), final)
    values[slots] = jnp.zeros((BS, BS), BF16)
    fwd_groups = group_count(slots, slab_blocks, FWD_GROUP, FWD_UNROLL)
    bwd_groups = group_count(slots, col_blocks, BWD_GROUP, BWD_PARTS * BWD_UNROLL)
    for copy in load_index:
        copy.wait()
    live = iota((1, slots), 1) < live_ref[...]
    lists_vmem[0] = sorted_lists(
        rows_ref[0], cols_ref[0], live, slab_blocks, col_blocks, FWD_GROUP, fwd_groups
    )
    fetch_fwd = pltpu.make_async_copy(lists_vmem.at[0], fwd_list, local_sem.at[8])
    fetch_fwd.start()
    for d in reversed(x_steps):
        a_x[d].wait_recv()
        for s, to in ways:
            a_hop[s, 1, d] = share(shard(z, at_x(-d), 0), to)
    a_final = 0
    for h in range(1, half_z + 1):
        for s, to in ways:
            b_hop[s, h].wait_recv()
            piece = shard(at_z(-s * h), x, 1)
            if h + 1 < half_z:
                b_hop[s, h + 1] = share(piece, to)
            elif h + 1 == half_z:
                b_hop[s, h + 1] = share(piece.at[halves[s]], to)
            else:
                piece = piece.at[halves[s]]
            for d in x_steps:
                share(piece, device(z, at_x(d), y, k), final)
        for d in range(X):
            for s, to in ways:
                if h < half_z:
                    a_hop[s, h, d].wait_recv()
                    piece = shard(at_z(-s * h), at_x(-d), 0)
                    if h + 1 < half_z:
                        a_hop[s, h + 1, d] = share(piece, to)
                    elif (d < half_x) == (s > 0):
                        share(piece, to, final)
                        a_final += 1
    wait_group(panel.at[pl.ds(0, a_final + Z * (X - 1))], final)
    fetch_fwd.wait()
    load_values.wait()

    zero_block = jnp.zeros((BS, BS), F32)

    def run_groups(table, group, first, groups, unroll, left, right, total):
        def step(base, total):
            for u in range(unroll):
                t = first + base * unroll + u
                at = t * group
                lhs = [left(at + g) for g in range(group)]
                rhs = [right(at + g) for g in range(group)]
                product = jnp.dot(
                    jnp.concatenate(lhs, axis=1),
                    jnp.concatenate(rhs, axis=0),
                    preferred_element_type=F32,
                )
                total = product + total * table[2, t].astype(F32)
                sums[t] = total
            return total

        assert groups % unroll == 0
        return lax.fori_loop(0, groups // unroll, step, total)

    run_groups(
        fwd_list,
        FWD_GROUP,
        0,
        fwd_groups,
        FWD_UNROLL,
        lambda at: values[fwd_list[0, at]],
        lambda at: panel[fwd_list[1, at]],
        zero_block,
    )
    sums[fwd_groups] = zero_block

    drain()

    def row_pair(yy, kk, i):
        return sums[fwd_list[3, 2 * (yy * K + kk) + i]]

    y_steps = sorted(range(1, Y), key=lambda d: -min(d, Y - d))
    from_core = {}
    for d in y_steps + [0]:
        for i in range(2):
            core_out[d, i] = row_pair(at_y(d), 1 - k, i).astype(BF16)
        from_core[d] = send(core_out.at[d], core_in.at[d], other_core)
    from_y = {}
    for d in y_steps:
        from_core[d].wait_recv()
        for i in range(2):
            y_out[d, i] = (row_pair(at_y(d), k, i) + core_in[d, i].astype(F32)).astype(BF16)
        from_y[d] = send(y_out.at[d], y_in.at[d], device(z, x, at_y(d), k))
    lists_vmem[1] = sorted_lists(
        cols_ref[0], rows_ref[0], live, col_blocks, slab_blocks, BWD_GROUP, bwd_groups
    )
    fetch_bwd = pltpu.make_async_copy(lists_vmem.at[1], bwd_list, local_sem.at[9])
    fetch_bwd.start()
    from_core[0].wait_recv()
    own = [row_pair(y, k, i) + core_in[0, i].astype(F32) for i in range(2)]
    for d in y_steps:
        from_y[d].wait_recv()
        for i in range(2):
            own[i] = own[i] + y_in[d, i].astype(F32)
    aggregate = jnp.concatenate(own, axis=0).astype(BF16)

    for copy in load_layer:
        copy.wait()
    weights = weights_ref[...]
    preact = jnp.dot(aggregate, weights, preferred_element_type=F32) + bias_ref[...]
    sigma = 1.0 / (1.0 + jnp.exp(-preact))
    deriv = sigma * (1.0 + preact * (1.0 - sigma))
    grad_pre_wide = cotangent_ref[...].astype(F32) * deriv
    grad_pre = grad_pre_wide.astype(BF16)
    grad_t = lax.dot_general(
        weights, grad_pre, (((1,), (1,)), ((), ())), preferred_element_type=F32
    ).astype(BF16)
    agg_t[2 * c] = grad_t[:, 0:BS]
    agg_t[2 * c + 1] = grad_t[:, BS : 2 * BS]

    def slab_pair(yy, kk):
        return agg_t.at[pl.ds(2 * (yy * K + kk), 2)]

    from_y = {}
    for d in y_steps:
        from_y[d] = share(slab_pair(y, k), device(z, x, at_y(d), k))
    core_slot = receive_slot()
    share(slab_pair(y, k), other_core, core_slot)
    hidden_ref[...] = (preact * sigma).astype(BF16)
    weight_term = lax.dot_general(
        aggregate, grad_pre, (((0,), (0,)), ((), ())), preferred_element_type=F32
    )
    bias_term = jnp.sum(grad_pre.astype(F32), axis=0, keepdims=True)
    grad_weights_ref[...] = weight_term
    rows_core = BS // K
    rows_y = rows_core // Y
    w_tall = rows_y + 8
    rows_x = w_z.shape[1]

    def rows_at(start, size):
        return pl.ds(pl.multiple_of(start, 8), size)

    for i, kk in ((0, 1 - k), (1, k)):
        w_half[i, 0:rows_core] = grad_weights_ref[rows_at(kk * rows_core, rows_core), :]
        w_half[i, rows_core : rows_core + 8] = jnp.broadcast_to(bias_term, (8, bias_term.shape[1]))
    w_core = stage([(w_half.at[0], w_half_in, other_core)], w_half_in)
    for d in reversed(y_steps):
        from_y[d].wait_recv()
        share(slab_pair(at_y(-d), k), other_core, core_slot)
    w_core.wait_recv()
    w_half[1] = w_half[1] + w_half_in[...]
    bias_rows = w_half[1, rows_core : rows_core + 8]
    for d in range(Y):
        w_y[d, 0:rows_y] = w_half[1, rows_at(at_y(d) * rows_y, rows_y), :]
        w_y[d, rows_y:w_tall] = bias_rows
    w_from_y = stage(
        [(w_y.at[d], w_y_in.at[y], device(z, x, at_y(d), k)) for d in y_steps],
        w_y_in.at[pl.ds(0, Y - 1)],
    )
    w_y_in[y] = w_y[0]
    wait_group(agg_t.at[pl.ds(0, 2 * Y)], core_slot)
    drain()

    w_copies = {}

    def stage_x():
        w_from_y.wait_recv()
        total = w_y_in[0]
        for yy in range(1, Y):
            total = total + w_y_in[yy]
        w_x[0:w_tall] = total
        if rows_x * X > w_tall:
            w_x[w_tall : rows_x * X] = jnp.zeros((rows_x * X - w_tall, total.shape[1]), F32)
        w_copies["x"] = stage(
            [
                (w_x.at[rows_at(at_x(d) * rows_x, rows_x)], w_x_in.at[x], device(z, at_x(d), y, k))
                for d in x_steps
            ],
            w_x_in.at[pl.ds(0, X - 1)],
        )
        w_x_in[x] = w_x[rows_at(x * rows_x, rows_x), :]

    def stage_z():
        w_copies["x"].wait_recv()
        total = w_x_in[0]
        for xx in range(1, X):
            total = total + w_x_in[xx]
        w_z[z] = total
        w_copies["z"] = stage(
            [(w_z.at[z], w_z.at[z], peer) for peer in z_peers], w_z.at[pl.ds(0, Z - 1)]
        )

    def stage_back_x():
        w_copies["z"].wait_recv()
        total = w_z[0]
        for zz in range(1, Z):
            total = total + w_z[zz]
        w_row[rows_at(x * rows_x, rows_x), :] = total
        mine = w_row.at[rows_at(x * rows_x, rows_x)]
        w_copies["bx"] = stage(
            [(mine, mine, device(z, at_x(d), y, k)) for d in x_steps],
            w_row.at[pl.ds(0, rows_x * (X - 1))],
        )

    def stage_back_y():
        w_copies["bx"].wait_recv()
        mine = rows_at(k * rows_core + y * rows_y, rows_y)
        w_full[mine, :] = w_row[0:rows_y]
        w_copies["by"] = stage(
            [(w_full.at[mine], w_full.at[mine], device(z, x, at_y(d), k)) for d in y_steps],
            w_full.at[pl.ds(0, rows_y * (Y - 1))],
        )

    def stage_back_core():
        w_copies["by"].wait_recv()
        mine = rows_at(k * rows_core, rows_core)
        w_copies["bc"] = stage([(w_full.at[mine], w_full.at[mine], other_core)], w_full.at[mine])

    stages = [stage_back_x, stage_back_y, stage_back_core]

    fetch_bwd.wait()
    part_groups = bwd_groups // BWD_PARTS
    running = zero_block
    for part in range(BWD_PARTS):
        running = run_groups(
            bwd_list,
            BWD_GROUP,
            part * part_groups,
            part_groups,
            BWD_UNROLL,
            lambda at: agg_t[bwd_list[1, at]],
            lambda at: values[bwd_list[0, at]],
            running,
        )
        (stage_x, stage_z)[part]()
    sums[bwd_groups] = zero_block

    def column(zz, xx, part):
        return sums[bwd_list[3, 2 * (zz * X + xx) + part]]

    a_hop = {}
    b_hop = {}
    b_x = {}
    x_slot = receive_slot()

    def send_a(s, to, h, d):
        if h == 1 and (d < half_x) != (s > 0):
            return
        i = 0 if s > 0 else 1
        total = column(at_z(s * (half_z - h + 1)), at_x(d), 0)
        if (s, h - 1, d) in a_hop:
            a_hop[s, h - 1, d].wait_recv()
            total = total + a_in[i, h - 2, d].astype(F32)
        a_out[i, h - 1, d] = total.astype(BF16)
        a_hop[s, h, d] = send(a_out.at[i, h - 1, d], a_in.at[i, h - 1, d], to)

    def send_bx(dz):
        b_x[dz % Z] = receive_slot()
        for i, d in enumerate(x_steps):
            bx_out[dz % Z, i] = column(at_z(dz), at_x(d), 1).astype(BF16)
            send(bx_out.at[dz % Z, i], bx_in.at[dz % Z, i], device(z, at_x(d), y, k), b_x[dz % Z])

    def sum_bx(dz):
        total = column(at_z(dz), x, 1)
        wait_group(bx_in.at[dz % Z, pl.ds(0, X - 1)], b_x[dz % Z])
        for i in range(X - 1):
            total = total + bx_in[dz % Z, i].astype(F32)
        return total

    def send_b(h):
        shared = sum_bx(half_z) if h == 1 else None
        for i, (s, to) in enumerate(ways):
            rows = slice(0, BS // 2) if s > 0 else slice(BS // 2, BS)
            if h == 1:
                b_out[i, 0, rows] = shared[rows].astype(BF16)
                b_hop[s, 1] = send(b_out.at[i, 0, halves[s]], b_in.at[i, 0, halves[s]], to)
                continue
            total = sum_bx(s * (half_z - h + 1))
            b_hop[s, h - 1].wait_recv()
            if h == 2:
                part = total[rows] + b_in[i, 0, rows].astype(F32)
                rest = total[BS // 2 : BS] if s > 0 else total[0 : BS // 2]
                total = jnp.concatenate([part, rest] if s > 0 else [rest, part], axis=0)
            else:
                total = total + b_in[i, h - 2].astype(F32)
            b_out[i, h - 1] = total.astype(BF16)
            b_hop[s, h] = send(b_out.at[i, h - 1], b_in.at[i, h - 1], to)

    for d in range(X):
        for s, to in ways:
            send_a(s, to, 1, d)
    send_bx(half_z)
    for h in range(half_z - 1, 1, -1):
        send_bx(h)
        send_bx(-h)
    for h in range(2, half_z + 1):
        for d in range(X):
            for s, to in ways:
                send_a(s, to, h, d)
        send_b(h - 1)
        if stages:
            stages.pop(0)()
        if h == 2:
            for near in (1, -1, 0):
                send_bx(near)
    last_a = None
    for i, d in enumerate(x_steps + [0]):
        total = column(z, at_x(d), 0)
        for j, (s, _) in enumerate(ways):
            a_hop[s, half_z, d].wait_recv()
            total = total + a_in[j, half_z - 1, d].astype(F32)
        if d:
            ax_out[i] = total.astype(BF16)
            send(ax_out.at[i], ax_in.at[i], device(z, at_x(d), y, k), x_slot)
        else:
            last_a = total
    send_b(half_z)
    while stages:
        stages.pop(0)()
    last_b = sum_bx(0)
    wait_group(ax_in.at[pl.ds(0, X - 1)], x_slot)
    for i in range(X - 1):
        last_a = last_a + ax_in[i].astype(F32)
    grad_features_ref[0:BS, :] = last_a.T
    grad_bias_ref[...] = w_row[rows_y : rows_y + 1] * scale
    w_copies["bc"].wait_recv()
    grad_weights_ref[...] = w_full[...] * scale
    drain()
    for i, (s, _) in enumerate(ways):
        b_hop[s, half_z].wait_recv()
        last_b = last_b + b_in[i, half_z - 1].astype(F32)
    grad_features_ref[BS : 2 * BS, :] = last_b.T
    for copy in staged:
        copy.wait_send()


def mesh_dims(mesh):
    rows, rep = mesh.shape["rows"], mesh.shape["rep"]
    across = 4 if rows >= 32 else 2
    return rows // across, across, rep // 2, 2


def shards(
    dims, features, weights, bias_vector, block_values, block_rows, block_cols, block_live, cotangent
):
    Z, X, Y, K = dims
    nodes, width = features.shape
    hid = weights.shape[1]
    slots = block_values.shape[2]
    half_z = Z // 2
    groups = max(
        group_count(slots, 2 * Y * K, FWD_GROUP, FWD_UNROLL),
        group_count(slots, 2 * Z * X, BWD_GROUP, BWD_PARTS * BWD_UNROLL),
    )
    rows_y = BS // K // Y
    rows_x = -(-(rows_y + 8) // (8 * X)) * 8
    scale = 1.0 / math.sqrt(nodes * Z * X * Y * K)
    vmem = pl.BlockSpec(memory_space=pltpu.VMEM)
    hbm = pl.BlockSpec(memory_space=pltpu.HBM)
    block = (BS, BS)
    out = pl.pallas_call(
        functools.partial(kernel, dims, scale),
        out_shape=(
            pltpu.VMEM((nodes, hid), BF16),
            pltpu.VMEM((nodes, width), F32),
            pltpu.VMEM((width, hid), F32),
            pltpu.VMEM((1, hid), F32),
        ),
        in_specs=[
            hbm,
            hbm,
            hbm,
            hbm,
            hbm,
            hbm,
            vmem,
            hbm,
        ],
        out_specs=(vmem, vmem, vmem, vmem),
        scratch_shapes=[
            pltpu.SMEM((8, LIST_WIDTH), jnp.int32),
            pltpu.SMEM((8, LIST_WIDTH), jnp.int32),
            pltpu.VMEM((2, 8, LIST_WIDTH), jnp.int32),
            pltpu.VMEM(block_rows.shape, jnp.int32),
            pltpu.VMEM(block_cols.shape, jnp.int32),
            pltpu.VMEM((slots + 1, *block), BF16),
            pltpu.VMEM((width, hid), BF16),
            pltpu.VMEM((1, hid), F32),
            pltpu.VMEM((nodes, hid), BF16),
            pltpu.VMEM((2 * Z * X, *block), BF16),
            pltpu.VMEM((groups + 1, *block), F32),
            pltpu.VMEM((Y, 2, *block), BF16),
            pltpu.VMEM((Y, 2, *block), BF16),
            pltpu.VMEM((Y, 2, *block), BF16),
            pltpu.VMEM((Y, 2, *block), BF16),
            pltpu.VMEM((2 * Y * K, *block), BF16),
            pltpu.VMEM((2, half_z, X, *block), BF16),
            pltpu.VMEM((2, half_z, X, *block), BF16),
            pltpu.VMEM((X, *block), BF16),
            pltpu.VMEM((X, *block), BF16),
            pltpu.VMEM((Z, X, *block), BF16),
            pltpu.VMEM((Z, X, *block), BF16),
            pltpu.VMEM((2, half_z, *block), BF16),
            pltpu.VMEM((2, half_z, *block), BF16),
            pltpu.VMEM((2, BS // K + 8, hid), F32),
            pltpu.VMEM((BS // K + 8, hid), F32),
            pltpu.VMEM((Y, rows_y + 8, hid), F32),
            pltpu.VMEM((Y, rows_y + 8, hid), F32),
            pltpu.VMEM((rows_x * X, hid), F32),
            pltpu.VMEM((X, rows_x, hid), F32),
            pltpu.VMEM((Z, rows_x, hid), F32),
            pltpu.VMEM((rows_x * X, hid), F32),
            pltpu.VMEM((BS, hid), F32),
            pltpu.SemaphoreType.DMA((SEND_SLOTS,)),
            pltpu.SemaphoreType.DMA((RECV_SLOTS,)),
            pltpu.SemaphoreType.DMA((STAGES,)),
            pltpu.SemaphoreType.DMA((10,)),
        ],
        compiler_params=pltpu.CompilerParams(
            collective_id=0, has_side_effects=True, vmem_limit_bytes=63 * 1024 * 1024
        ),
        name="layer",
    )(
        features,
        weights,
        bias_vector.reshape(1, hid),
        block_values,
        block_rows,
        block_cols,
        block_live,
        cotangent,
    )
    hidden, grad_features, grad_weights, grad_bias = out
    return hidden, grad_features, grad_weights, grad_bias.reshape(hid)


def solution(mesh):
    in_specs = (
        P(("rows", "rep"), None),
        P(),
        P(),
        P("rows", "rep", None, None, None),
        P("rows", "rep", None),
        P("rows", "rep", None),
        P("rows", "rep"),
        P(("rows", "rep"), None),
    )
    out_specs = (P(("rows", "rep"), None), P(("rows", "rep"), None), P(), P())
    return jax.shard_map(
        functools.partial(shards, mesh_dims(mesh)),
        mesh=mesh,
        in_specs=in_specs,
        out_specs=out_specs,
        check_vma=False,
    )
```

```python
import functools
import math

import jax
import jax.numpy as jnp
from jax import lax
from jax.experimental import pallas as pl
from jax.experimental.pallas import tpu as pltpu
from jax.sharding import PartitionSpec as P

MESH = pl.DeviceIdType.MESH
F32 = jnp.float32
BF16 = jnp.bfloat16
BS = 128
FWD_GROUP = 4
BWD_GROUP = 2
FWD_UNROLL = 46
BWD_UNROLL = 48
BWD_PARTS = 2
SEND_SLOTS = 3
RECV_SLOTS = 99
STAGES = 7
LIST_WIDTH = 384


def group_count(slots, keys, group, unroll):
    groups = (slots + keys * (group - 1)) // group
    return -(-groups // unroll) * unroll


def iota(shape, dim):
    return lax.broadcasted_iota(jnp.int32, shape, dim)


def sorted_lists(key, other, live, keys, partners, group, groups):
    slots = key.shape[1]
    shift = group.bit_length() - 1
    picked = (iota((keys, slots), 0) == key) & live
    one_hot = jnp.where(picked, 1.0, 0.0).astype(F32)
    before = jnp.where(iota((slots, slots), 0) < iota((slots, slots), 1), 1.0, 0.0).astype(BF16)
    place = jnp.dot(one_hot.astype(BF16), before, preferred_element_type=F32)
    count = jnp.sum(one_hot, axis=1, keepdims=True).astype(jnp.int32)
    runs = lax.shift_right_logical(count + (group - 1), shift)
    lower = jnp.where(iota((keys, keys), 1) < iota((keys, keys), 0), 1.0, 0.0).astype(BF16)
    wide_runs = jnp.broadcast_to(runs, (keys, 128)).astype(F32).astype(BF16)
    start = jnp.dot(lower, wide_runs, preferred_element_type=F32)[:, :1]
    target = jnp.sum(one_hot * (start * group + place), axis=0, keepdims=True).astype(jnp.int32)
    target = jnp.where(live, target, -1)
    match = jnp.where(iota((LIST_WIDTH, slots), 0) == target, 1.0, 0.0).astype(BF16)
    number = iota((8, slots), 1)
    line = iota((8, slots), 0)
    facts = jnp.where(
        line == 0,
        lax.shift_right_logical(number, 4),
        jnp.where(line == 1, number & 15, jnp.where(line == 2, jnp.broadcast_to(other, (8, slots)), 1)),
    )
    found = lax.dot_general(
        facts.astype(F32).astype(BF16), match, (((1,), (1,)), ((), ())), preferred_element_type=F32
    ).astype(jnp.int32)
    slot = found[0:1] * 16 + found[1:2] + (1 - found[3:4]) * slots
    partner = found[2:3]
    start_int = start.astype(jnp.int32)
    lane = iota((keys, LIST_WIDTH), 1)
    opens = jnp.sum(jnp.where((start_int == lane) & (count > 0), 1.0, 0.0), axis=0, keepdims=True)
    keep = 1 - opens.astype(jnp.int32)
    final = jnp.where(count > 0, start_int + runs - 1, groups).astype(F32)
    last = jnp.sum(jnp.where(iota((keys, LIST_WIDTH), 0) == lane, final, 0.0), axis=0, keepdims=True)
    out_line = iota((8, LIST_WIDTH), 0)
    slot = jnp.clip(slot, 0, slots)
    partner = jnp.clip(partner, 0, partners - 1)
    keep = jnp.clip(keep, 0, 1)
    last = jnp.clip(last.astype(jnp.int32), 0, groups)
    return jnp.where(
        out_line == 0,
        slot,
        jnp.where(out_line == 1, partner, jnp.where(out_line == 2, keep, last)),
    )


def kernel(
    dims,
    scale,
    features_hbm,
    weights_hbm,
    bias_hbm,
    values_hbm,
    rows_hbm,
    cols_hbm,
    live_ref,
    cotangent_hbm,
    hidden_ref,
    grad_features_ref,
    grad_weights_ref,
    grad_bias_ref,
    fwd_list,
    bwd_list,
    lists_vmem,
    rows_ref,
    cols_ref,
    values,
    weights_ref,
    bias_ref,
    cotangent_ref,
    panel,
    sums,
    core_out,
    core_in,
    y_out,
    y_in,
    agg_t,
    a_out,
    a_in,
    ax_out,
    ax_in,
    bx_out,
    bx_in,
    b_out,
    b_in,
    w_half,
    w_half_in,
    w_y,
    w_y_in,
    w_x,
    w_x_in,
    w_z,
    w_row,
    w_full,
    send_sem,
    recv_sem,
    stage_sem,
    local_sem,
):
    Z, X, Y, K = dims
    slots = values_hbm.shape[2]
    half_z = Z // 2
    half_x = X // 2
    slab_blocks = 2 * Y * K
    col_blocks = 2 * Z * X
    r = lax.axis_index("rows")
    c = lax.axis_index("rep")
    z, x, y, k = lax.div(r, X), lax.rem(r, X), lax.div(c, K), lax.rem(c, K)

    def at_z(step):
        return lax.rem(z + (step + Z), Z)

    def at_x(step):
        return lax.rem(x + (step + X), X)

    def at_y(step):
        return lax.rem(y + (step + Y), Y)

    def device(zz, xx, yy, kk):
        return (zz * X + xx, yy * K + kk)

    other_core = device(z, x, y, 1 - k)
    z_peers = [device(at_z(s), x, y, k) for s in range(1, Z)]
    x_peers = [device(z, at_x(s), y, k) for s in range(1, X)]
    y_peers = [device(z, x, at_y(s), k) for s in range(1, Y)]
    peers = [other_core] + z_peers + x_peers + y_peers

    barrier = pltpu.get_barrier_semaphore()
    for peer in peers:
        pl.semaphore_signal(barrier, inc=1, device_id=peer, device_id_type=MESH)

    load_values = pltpu.make_async_copy(
        values_hbm.at[0, 0], values.at[pl.ds(0, slots)], local_sem.at[0]
    )
    load_own = [
        pltpu.make_async_copy(
            features_hbm.at[pl.ds(i * BS, BS)], panel.at[2 * r + i], local_sem.at[1 + i]
        )
        for i in range(2)
    ]
    for copy in load_own:
        copy.start()
    load_values.start()
    load_layer = [
        pltpu.make_async_copy(weights_hbm, weights_ref, local_sem.at[3]),
        pltpu.make_async_copy(bias_hbm, bias_ref, local_sem.at[4]),
        pltpu.make_async_copy(cotangent_hbm, cotangent_ref, local_sem.at[5]),
    ]
    for copy in load_layer:
        copy.start()
    load_index = [
        pltpu.make_async_copy(rows_hbm, rows_ref, local_sem.at[6]),
        pltpu.make_async_copy(cols_hbm, cols_ref, local_sem.at[7]),
    ]
    for copy in load_index:
        copy.start()
    pl.semaphore_wait(barrier, len(peers))
    for copy in load_own:
        copy.wait()

    used = [0]
    bulk = [0, 0]
    staged = []

    def receive_slot():
        used[0] += 1
        return used[0] - 1

    def send(src, dst, to, slot=None, sent=None):
        if sent is None:
            sent = send_sem.at[bulk[0]]
            bulk[1] += math.prod(src.shape)
        copy = pltpu.make_async_remote_copy(
            src_ref=src,
            dst_ref=dst,
            send_sem=sent,
            recv_sem=recv_sem.at[receive_slot() if slot is None else slot],
            device_id=to,
            device_id_type=MESH,
        )
        copy.start()
        return copy

    def whole(ref, slot, sent):
        return pltpu.make_async_remote_copy(
            src_ref=ref,
            dst_ref=ref,
            send_sem=sent,
            recv_sem=recv_sem.at[slot],
            device_id=other_core,
            device_id_type=MESH,
        )

    def wait_group(ref, slot):
        whole(ref, slot, send_sem.at[0]).wait_recv()

    def drain():
        blocks = bulk[1] // (BS * BS)
        assert blocks * BS * BS == bulk[1] and blocks <= panel.shape[0]
        whole(panel.at[pl.ds(0, blocks)], 0, send_sem.at[bulk[0]]).wait_send()
        bulk[0] += 1
        bulk[1] = 0

    def share(piece, to, slot=None):
        return send(piece, piece, to, slot)

    def stage(copies, ref):
        slot = receive_slot()
        sent = stage_sem.at[len(staged)]
        for src, dst, to in copies:
            send(src, dst, to, slot, sent)
        staged.append(whole(ref, slot, sent))
        return staged[-1]

    up, down = device(at_z(1), x, y, k), device(at_z(-1), x, y, k)
    ways = ((1, up), (-1, down))
    x_steps = sorted(range(1, X), key=lambda d: -min(d, X - d))

    def shard(zz, xx, part):
        return panel.at[2 * (zz * X + xx) + part]

    halves = {1: pl.ds(0, BS // 2), -1: pl.ds(BS // 2, BS // 2)}
    final = receive_slot()

    a_x = {}
    for d in x_steps:
        a_x[d] = share(shard(z, x, 0), device(z, at_x(d), y, k))
    a_hop = {}
    b_hop = {}
    for s, to in ways:
        a_hop[s, 1, 0] = share(shard(z, x, 0), to)
        b_hop[s, 1] = share(shard(z, x, 1), to)
    for d in x_steps:
        share(shard(z, x, 1), device(z, at_x(d), y, k), final)
    values[slots] = jnp.zeros((BS, BS), BF16)
    fwd_groups = group_count(slots, slab_blocks, FWD_GROUP, FWD_UNROLL)
    bwd_groups = group_count(slots, col_blocks, BWD_GROUP, BWD_PARTS * BWD_UNROLL)
    for copy in load_index:
        copy.wait()
    live = iota((1, slots), 1) < live_ref[...]
    lists_vmem[0] = sorted_lists(
        rows_ref[0], cols_ref[0], live, slab_blocks, col_blocks, FWD_GROUP, fwd_groups
    )
    fetch_fwd = pltpu.make_async_copy(lists_vmem.at[0], fwd_list, local_sem.at[8])
    fetch_fwd.start()
    for d in reversed(x_steps):
        a_x[d].wait_recv()
        for s, to in ways:
            a_hop[s, 1, d] = share(shard(z, at_x(-d), 0), to)
    a_final = 0
    for h in range(1, half_z + 1):
        for s, to in ways:
            b_hop[s, h].wait_recv()
            piece = shard(at_z(-s * h), x, 1)
            if h + 1 < half_z:
                b_hop[s, h + 1] = share(piece, to)
            elif h + 1 == half_z:
                b_hop[s, h + 1] = share(piece.at[halves[s]], to)
            else:
                piece = piece.at[halves[s]]
            for d in x_steps:
                share(piece, device(z, at_x(d), y, k), final)
        for d in range(X):
            for s, to in ways:
                if h < half_z:
                    a_hop[s, h, d].wait_recv()
                    piece = shard(at_z(-s * h), at_x(-d), 0)
                    if h + 1 < half_z:
                        a_hop[s, h + 1, d] = share(piece, to)
                    elif (d < half_x) == (s > 0):
                        share(piece, to, final)
                        a_final += 1
    wait_group(panel.at[pl.ds(0, a_final + Z * (X - 1))], final)
    fetch_fwd.wait()
    load_values.wait()

    zero_block = jnp.zeros((BS, BS), F32)

    def run_groups(table, group, first, groups, unroll, left, right, total):
        def step(base, total):
            for u in range(unroll):
                t = first + base * unroll + u
                at = t * group
                lhs = [left(at + g) for g in range(group)]
                rhs = [right(at + g) for g in range(group)]
                product = jnp.dot(
                    jnp.concatenate(lhs, axis=1),
                    jnp.concatenate(rhs, axis=0),
                    preferred_element_type=F32,
                )
                total = product + total * table[2, t].astype(F32)
                sums[t] = total
            return total

        assert groups % unroll == 0
        return lax.fori_loop(0, groups // unroll, step, total)

    run_groups(
        fwd_list,
        FWD_GROUP,
        0,
        fwd_groups,
        FWD_UNROLL,
        lambda at: values[fwd_list[0, at]],
        lambda at: panel[fwd_list[1, at]],
        zero_block,
    )
    sums[fwd_groups] = zero_block

    drain()

    def row_pair(yy, kk, i):
        return sums[fwd_list[3, 2 * (yy * K + kk) + i]]

    y_steps = sorted(range(1, Y), key=lambda d: -min(d, Y - d))
    from_core = {}
    for d in y_steps + [0]:
        for i in range(2):
            core_out[d, i] = row_pair(at_y(d), 1 - k, i).astype(BF16)
        from_core[d] = send(core_out.at[d], core_in.at[d], other_core)
    from_y = {}
    for d in y_steps:
        from_core[d].wait_recv()
        for i in range(2):
            y_out[d, i] = (row_pair(at_y(d), k, i) + core_in[d, i].astype(F32)).astype(BF16)
        from_y[d] = send(y_out.at[d], y_in.at[d], device(z, x, at_y(d), k))
    lists_vmem[1] = sorted_lists(
        cols_ref[0], rows_ref[0], live, col_blocks, slab_blocks, BWD_GROUP, bwd_groups
    )
    fetch_bwd = pltpu.make_async_copy(lists_vmem.at[1], bwd_list, local_sem.at[9])
    fetch_bwd.start()
    from_core[0].wait_recv()
    own = [row_pair(y, k, i) + core_in[0, i].astype(F32) for i in range(2)]
    for d in y_steps:
        from_y[d].wait_recv()
        for i in range(2):
            own[i] = own[i] + y_in[d, i].astype(F32)
    aggregate = jnp.concatenate(own, axis=0).astype(BF16)

    for copy in load_layer:
        copy.wait()
    weights = weights_ref[...]
    preact = jnp.dot(aggregate, weights, preferred_element_type=F32) + bias_ref[...]
    sigma = 1.0 / (1.0 + jnp.exp(-preact))
    deriv = sigma * (1.0 + preact * (1.0 - sigma))
    grad_pre_wide = cotangent_ref[...].astype(F32) * deriv
    grad_pre = grad_pre_wide.astype(BF16)
    grad_t = lax.dot_general(
        weights, grad_pre, (((1,), (1,)), ((), ())), preferred_element_type=F32
    ).astype(BF16)
    agg_t[2 * c] = grad_t[:, 0:BS]
    agg_t[2 * c + 1] = grad_t[:, BS : 2 * BS]

    def slab_pair(yy, kk):
        return agg_t.at[pl.ds(2 * (yy * K + kk), 2)]

    from_y = {}
    for d in y_steps:
        from_y[d] = share(slab_pair(y, k), device(z, x, at_y(d), k))
    core_slot = receive_slot()
    share(slab_pair(y, k), other_core, core_slot)
    hidden_ref[...] = (preact * sigma).astype(BF16)
    weight_term = lax.dot_general(
        aggregate, grad_pre, (((0,), (0,)), ((), ())), preferred_element_type=F32
    )
    bias_term = jnp.sum(grad_pre.astype(F32), axis=0, keepdims=True)
    grad_weights_ref[...] = weight_term
    rows_core = BS // K
    rows_y = rows_core // Y
    w_tall = rows_y + 8
    rows_x = w_z.shape[1]

    def rows_at(start, size):
        return pl.ds(pl.multiple_of(start, 8), size)

    for i, kk in ((0, 1 - k), (1, k)):
        w_half[i, 0:rows_core] = grad_weights_ref[rows_at(kk * rows_core, rows_core), :]
        w_half[i, rows_core : rows_core + 8] = jnp.broadcast_to(bias_term, (8, bias_term.shape[1]))
    w_core = stage([(w_half.at[0], w_half_in, other_core)], w_half_in)
    for d in reversed(y_steps):
        from_y[d].wait_recv()
        share(slab_pair(at_y(-d), k), other_core, core_slot)
    w_core.wait_recv()
    w_half[1] = w_half[1] + w_half_in[...]
    bias_rows = w_half[1, rows_core : rows_core + 8]
    for d in range(Y):
        w_y[d, 0:rows_y] = w_half[1, rows_at(at_y(d) * rows_y, rows_y), :]
        w_y[d, rows_y:w_tall] = bias_rows
    w_from_y = stage(
        [(w_y.at[d], w_y_in.at[y], device(z, x, at_y(d), k)) for d in y_steps],
        w_y_in.at[pl.ds(0, Y - 1)],
    )
    w_y_in[y] = w_y[0]
    wait_group(agg_t.at[pl.ds(0, 2 * Y)], core_slot)

    w_copies = {}

    def stage_x():
        w_from_y.wait_recv()
        total = w_y_in[0]
        for yy in range(1, Y):
            total = total + w_y_in[yy]
        w_x[0:w_tall] = total
        if rows_x * X > w_tall:
            w_x[w_tall : rows_x * X] = jnp.zeros((rows_x * X - w_tall, total.shape[1]), F32)
        w_copies["x"] = stage(
            [
                (w_x.at[rows_at(at_x(d) * rows_x, rows_x)], w_x_in.at[x], device(z, at_x(d), y, k))
                for d in x_steps
            ],
            w_x_in.at[pl.ds(0, X - 1)],
        )
        w_x_in[x] = w_x[rows_at(x * rows_x, rows_x), :]

    def stage_z():
        w_copies["x"].wait_recv()
        total = w_x_in[0]
        for xx in range(1, X):
            total = total + w_x_in[xx]
        w_z[z] = total
        w_copies["z"] = stage(
            [(w_z.at[z], w_z.at[z], peer) for peer in z_peers], w_z.at[pl.ds(0, Z - 1)]
        )

    def stage_back_x():
        w_copies["z"].wait_recv()
        total = w_z[0]
        for zz in range(1, Z):
            total = total + w_z[zz]
        w_row[rows_at(x * rows_x, rows_x), :] = total
        mine = w_row.at[rows_at(x * rows_x, rows_x)]
        w_copies["bx"] = stage(
            [(mine, mine, device(z, at_x(d), y, k)) for d in x_steps],
            w_row.at[pl.ds(0, rows_x * (X - 1))],
        )

    def stage_back_y():
        w_copies["bx"].wait_recv()
        mine = rows_at(k * rows_core + y * rows_y, rows_y)
        w_full[mine, :] = w_row[0:rows_y]
        w_copies["by"] = stage(
            [(w_full.at[mine], w_full.at[mine], device(z, x, at_y(d), k)) for d in y_steps],
            w_full.at[pl.ds(0, rows_y * (Y - 1))],
        )

    def stage_back_core():
        w_copies["by"].wait_recv()
        mine = rows_at(k * rows_core, rows_core)
        w_copies["bc"] = stage([(w_full.at[mine], w_full.at[mine], other_core)], w_full.at[mine])

    stages = [stage_z, stage_back_x, stage_back_y, stage_back_core]

    fetch_bwd.wait()
    part_groups = bwd_groups // BWD_PARTS
    running = zero_block
    for part in range(BWD_PARTS):
        running = run_groups(
            bwd_list,
            BWD_GROUP,
            part * part_groups,
            part_groups,
            BWD_UNROLL,
            lambda at: agg_t[bwd_list[1, at]],
            lambda at: values[bwd_list[0, at]],
            running,
        )
        if part == 0:
            stage_x()
            drain()
    sums[bwd_groups] = zero_block

    def column(zz, xx, part):
        return sums[bwd_list[3, 2 * (zz * X + xx) + part]]

    a_hop = {}
    b_hop = {}
    b_x = {}
    x_slot = receive_slot()

    def send_a(s, to, h, d):
        if h == 1 and (d < half_x) != (s > 0):
            return
        i = 0 if s > 0 else 1
        total = column(at_z(s * (half_z - h + 1)), at_x(d), 0)
        if (s, h - 1, d) in a_hop:
            a_hop[s, h - 1, d].wait_recv()
            total = total + a_in[i, h - 2, d].astype(F32)
        a_out[i, h - 1, d] = total.astype(BF16)
        a_hop[s, h, d] = send(a_out.at[i, h - 1, d], a_in.at[i, h - 1, d], to)

    def send_bx(dz):
        b_x[dz % Z] = receive_slot()
        for i, d in enumerate(x_steps):
            bx_out[dz % Z, i] = column(at_z(dz), at_x(d), 1).astype(BF16)
            send(bx_out.at[dz % Z, i], bx_in.at[dz % Z, i], device(z, at_x(d), y, k), b_x[dz % Z])

    def sum_bx(dz):
        total = column(at_z(dz), x, 1)
        wait_group(bx_in.at[dz % Z, pl.ds(0, X - 1)], b_x[dz % Z])
        for i in range(X - 1):
            total = total + bx_in[dz % Z, i].astype(F32)
        return total

    def send_b(h):
        shared = sum_bx(half_z) if h == 1 else None
        for i, (s, to) in enumerate(ways):
            rows = slice(0, BS // 2) if s > 0 else slice(BS // 2, BS)
            if h == 1:
                b_out[i, 0, rows] = shared[rows].astype(BF16)
                b_hop[s, 1] = send(b_out.at[i, 0, halves[s]], b_in.at[i, 0, halves[s]], to)
                continue
            total = sum_bx(s * (half_z - h + 1))
            b_hop[s, h - 1].wait_recv()
            if h == 2:
                part = total[rows] + b_in[i, 0, rows].astype(F32)
                rest = total[BS // 2 : BS] if s > 0 else total[0 : BS // 2]
                total = jnp.concatenate([part, rest] if s > 0 else [rest, part], axis=0)
            else:
                total = total + b_in[i, h - 2].astype(F32)
            b_out[i, h - 1] = total.astype(BF16)
            b_hop[s, h] = send(b_out.at[i, h - 1], b_in.at[i, h - 1], to)

    for d in range(X):
        for s, to in ways:
            send_a(s, to, 1, d)
    send_bx(half_z)
    for h in range(half_z - 1, 1, -1):
        send_bx(h)
        send_bx(-h)
        if h == half_z - 1:
            stages.pop(0)()
    for h in range(2, half_z + 1):
        for d in range(X):
            for s, to in ways:
                send_a(s, to, h, d)
        send_b(h - 1)
        if stages:
            stages.pop(0)()
        if h == 2:
            for near in (1, -1, 0):
                send_bx(near)
    last_a = None
    for i, d in enumerate(x_steps + [0]):
        total = column(z, at_x(d), 0)
        for j, (s, _) in enumerate(ways):
            a_hop[s, half_z, d].wait_recv()
            total = total + a_in[j, half_z - 1, d].astype(F32)
        if d:
            ax_out[i] = total.astype(BF16)
            send(ax_out.at[i], ax_in.at[i], device(z, at_x(d), y, k), x_slot)
        else:
            last_a = total
    send_b(half_z)
    while stages:
        stages.pop(0)()
    last_b = sum_bx(0)
    wait_group(ax_in.at[pl.ds(0, X - 1)], x_slot)
    for i in range(X - 1):
        last_a = last_a + ax_in[i].astype(F32)
    grad_features_ref[0:BS, :] = last_a.T
    grad_bias_ref[...] = w_row[rows_y : rows_y + 1] * scale
    w_copies["bc"].wait_recv()
    grad_weights_ref[...] = w_full[...] * scale
    drain()
    for i, (s, _) in enumerate(ways):
        b_hop[s, half_z].wait_recv()
        last_b = last_b + b_in[i, half_z - 1].astype(F32)
    grad_features_ref[BS : 2 * BS, :] = last_b.T
    for copy in staged:
        copy.wait_send()


def mesh_dims(mesh):
    rows, rep = mesh.shape["rows"], mesh.shape["rep"]
    across = 4 if rows >= 32 else 2
    return rows // across, across, rep // 2, 2


def shards(
    dims, features, weights, bias_vector, block_values, block_rows, block_cols, block_live, cotangent
):
    Z, X, Y, K = dims
    nodes, width = features.shape
    hid = weights.shape[1]
    slots = block_values.shape[2]
    half_z = Z // 2
    groups = max(
        group_count(slots, 2 * Y * K, FWD_GROUP, FWD_UNROLL),
        group_count(slots, 2 * Z * X, BWD_GROUP, BWD_PARTS * BWD_UNROLL),
    )
    rows_y = BS // K // Y
    rows_x = -(-(rows_y + 8) // (8 * X)) * 8
    scale = 1.0 / math.sqrt(nodes * Z * X * Y * K)
    vmem = pl.BlockSpec(memory_space=pltpu.VMEM)
    hbm = pl.BlockSpec(memory_space=pltpu.HBM)
    block = (BS, BS)
    out = pl.pallas_call(
        functools.partial(kernel, dims, scale),
        out_shape=(
            pltpu.VMEM((nodes, hid), BF16),
            pltpu.VMEM((nodes, width), F32),
            pltpu.VMEM((width, hid), F32),
            pltpu.VMEM((1, hid), F32),
        ),
        in_specs=[
            hbm,
            hbm,
            hbm,
            hbm,
            hbm,
            hbm,
            vmem,
            hbm,
        ],
        out_specs=(vmem, vmem, vmem, vmem),
        scratch_shapes=[
            pltpu.SMEM((8, LIST_WIDTH), jnp.int32),
            pltpu.SMEM((8, LIST_WIDTH), jnp.int32),
            pltpu.VMEM((2, 8, LIST_WIDTH), jnp.int32),
            pltpu.VMEM(block_rows.shape, jnp.int32),
            pltpu.VMEM(block_cols.shape, jnp.int32),
            pltpu.VMEM((slots + 1, *block), BF16),
            pltpu.VMEM((width, hid), BF16),
            pltpu.VMEM((1, hid), F32),
            pltpu.VMEM((nodes, hid), BF16),
            pltpu.VMEM((2 * Z * X, *block), BF16),
            pltpu.VMEM((groups + 1, *block), F32),
            pltpu.VMEM((Y, 2, *block), BF16),
            pltpu.VMEM((Y, 2, *block), BF16),
            pltpu.VMEM((Y, 2, *block), BF16),
            pltpu.VMEM((Y, 2, *block), BF16),
            pltpu.VMEM((2 * Y * K, *block), BF16),
            pltpu.VMEM((2, half_z, X, *block), BF16),
            pltpu.VMEM((2, half_z, X, *block), BF16),
            pltpu.VMEM((X, *block), BF16),
            pltpu.VMEM((X, *block), BF16),
            pltpu.VMEM((Z, X, *block), BF16),
            pltpu.VMEM((Z, X, *block), BF16),
            pltpu.VMEM((2, half_z, *block), BF16),
            pltpu.VMEM((2, half_z, *block), BF16),
            pltpu.VMEM((2, BS // K + 8, hid), F32),
            pltpu.VMEM((BS // K + 8, hid), F32),
            pltpu.VMEM((Y, rows_y + 8, hid), F32),
            pltpu.VMEM((Y, rows_y + 8, hid), F32),
            pltpu.VMEM((rows_x * X, hid), F32),
            pltpu.VMEM((X, rows_x, hid), F32),
            pltpu.VMEM((Z, rows_x, hid), F32),
            pltpu.VMEM((rows_x * X, hid), F32),
            pltpu.VMEM((BS, hid), F32),
            pltpu.SemaphoreType.DMA((SEND_SLOTS,)),
            pltpu.SemaphoreType.DMA((RECV_SLOTS,)),
            pltpu.SemaphoreType.DMA((STAGES,)),
            pltpu.SemaphoreType.DMA((10,)),
        ],
        compiler_params=pltpu.CompilerParams(
            collective_id=0, has_side_effects=True, vmem_limit_bytes=63 * 1024 * 1024
        ),
        name="layer",
    )(
        features,
        weights,
        bias_vector.reshape(1, hid),
        block_values,
        block_rows,
        block_cols,
        block_live,
        cotangent,
    )
    hidden, grad_features, grad_weights, grad_bias = out
    return hidden, grad_features, grad_weights, grad_bias.reshape(hid)


def solution(mesh):
    in_specs = (
        P(("rows", "rep"), None),
        P(),
        P(),
        P("rows", "rep", None, None, None),
        P("rows", "rep", None),
        P("rows", "rep", None),
        P("rows", "rep"),
        P(("rows", "rep"), None),
    )
    out_specs = (P(("rows", "rep"), None), P(("rows", "rep"), None), P(), P())
    return jax.shard_map(
        functools.partial(shards, mesh_dims(mesh)),
        mesh=mesh,
        in_specs=in_specs,
        out_specs=out_specs,
        check_vma=False,
    )
```

```python
import functools
import math

import jax
import jax.numpy as jnp
from jax import lax
from jax.experimental import pallas as pl
from jax.experimental.pallas import tpu as pltpu
from jax.sharding import PartitionSpec as P

MESH = pl.DeviceIdType.MESH
F32 = jnp.float32
BF16 = jnp.bfloat16
BS = 128
FWD_GROUP = 4
BWD_GROUP = 2
FWD_UNROLL = 46
BWD_UNROLL = 48
BWD_PARTS = 2
SEND_SLOTS = 3
RECV_SLOTS = 102
STAGES = 7
LIST_WIDTH = 384


def group_count(slots, keys, group, unroll):
    groups = (slots + keys * (group - 1)) // group
    return -(-groups // unroll) * unroll


def iota(shape, dim):
    return lax.broadcasted_iota(jnp.int32, shape, dim)


def sorted_lists(key, other, live, keys, partners, group, groups):
    slots = key.shape[1]
    shift = group.bit_length() - 1
    picked = (iota((keys, slots), 0) == key) & live
    one_hot = jnp.where(picked, 1.0, 0.0).astype(F32)
    before = jnp.where(iota((slots, slots), 0) < iota((slots, slots), 1), 1.0, 0.0).astype(BF16)
    place = jnp.dot(one_hot.astype(BF16), before, preferred_element_type=F32)
    count = jnp.sum(one_hot, axis=1, keepdims=True).astype(jnp.int32)
    runs = lax.shift_right_logical(count + (group - 1), shift)
    lower = jnp.where(iota((keys, keys), 1) < iota((keys, keys), 0), 1.0, 0.0).astype(BF16)
    wide_runs = jnp.broadcast_to(runs, (keys, 128)).astype(F32).astype(BF16)
    start = jnp.dot(lower, wide_runs, preferred_element_type=F32)[:, :1]
    target = jnp.sum(one_hot * (start * group + place), axis=0, keepdims=True).astype(jnp.int32)
    target = jnp.where(live, target, -1)
    match = jnp.where(iota((LIST_WIDTH, slots), 0) == target, 1.0, 0.0).astype(BF16)
    number = iota((8, slots), 1)
    line = iota((8, slots), 0)
    facts = jnp.where(
        line == 0,
        lax.shift_right_logical(number, 4),
        jnp.where(line == 1, number & 15, jnp.where(line == 2, jnp.broadcast_to(other, (8, slots)), 1)),
    )
    found = lax.dot_general(
        facts.astype(F32).astype(BF16), match, (((1,), (1,)), ((), ())), preferred_element_type=F32
    ).astype(jnp.int32)
    slot = found[0:1] * 16 + found[1:2] + (1 - found[3:4]) * slots
    partner = found[2:3]
    start_int = start.astype(jnp.int32)
    lane = iota((keys, LIST_WIDTH), 1)
    opens = jnp.sum(jnp.where((start_int == lane) & (count > 0), 1.0, 0.0), axis=0, keepdims=True)
    keep = 1 - opens.astype(jnp.int32)
    final = jnp.where(count > 0, start_int + runs - 1, groups).astype(F32)
    last = jnp.sum(jnp.where(iota((keys, LIST_WIDTH), 0) == lane, final, 0.0), axis=0, keepdims=True)
    out_line = iota((8, LIST_WIDTH), 0)
    slot = jnp.clip(slot, 0, slots)
    partner = jnp.clip(partner, 0, partners - 1)
    keep = jnp.clip(keep, 0, 1)
    last = jnp.clip(last.astype(jnp.int32), 0, groups)
    return jnp.where(
        out_line == 0,
        slot,
        jnp.where(out_line == 1, partner, jnp.where(out_line == 2, keep, last)),
    )


def kernel(
    dims,
    scale,
    features_hbm,
    weights_hbm,
    bias_hbm,
    values_hbm,
    rows_hbm,
    cols_hbm,
    live_ref,
    cotangent_hbm,
    hidden_ref,
    grad_features_ref,
    grad_weights_ref,
    grad_bias_ref,
    fwd_list,
    bwd_list,
    lists_vmem,
    rows_ref,
    cols_ref,
    values,
    weights_ref,
    bias_ref,
    cotangent_ref,
    panel,
    sums,
    core_out,
    core_in,
    y_out,
    y_in,
    agg_t,
    a_out,
    a_in,
    ax_out,
    ax_in,
    bx_out,
    bx_in,
    b_out,
    b_in,
    w_half,
    w_half_in,
    w_y,
    w_y_in,
    w_x,
    w_x_in,
    w_z,
    w_row,
    w_full,
    send_sem,
    recv_sem,
    stage_sem,
    local_sem,
):
    Z, X, Y, K = dims
    slots = values_hbm.shape[2]
    half_z = Z // 2
    half_x = X // 2
    slab_blocks = 2 * Y * K
    col_blocks = 2 * Z * X
    r = lax.axis_index("rows")
    c = lax.axis_index("rep")
    z, x, y, k = lax.div(r, X), lax.rem(r, X), lax.div(c, K), lax.rem(c, K)

    def at_z(step):
        return lax.rem(z + (step + Z), Z)

    def at_x(step):
        return lax.rem(x + (step + X), X)

    def at_y(step):
        return lax.rem(y + (step + Y), Y)

    def device(zz, xx, yy, kk):
        return (zz * X + xx, yy * K + kk)

    other_core = device(z, x, y, 1 - k)
    z_peers = [device(at_z(s), x, y, k) for s in range(1, Z)]
    x_peers = [device(z, at_x(s), y, k) for s in range(1, X)]
    y_peers = [device(z, x, at_y(s), k) for s in range(1, Y)]
    peers = [other_core] + z_peers + x_peers + y_peers

    barrier = pltpu.get_barrier_semaphore()
    for peer in peers:
        pl.semaphore_signal(barrier, inc=1, device_id=peer, device_id_type=MESH)

    load_values = pltpu.make_async_copy(
        values_hbm.at[0, 0], values.at[pl.ds(0, slots)], local_sem.at[0]
    )
    load_own = [
        pltpu.make_async_copy(
            features_hbm.at[pl.ds(i * BS, BS)], panel.at[2 * r + i], local_sem.at[1 + i]
        )
        for i in range(2)
    ]
    for copy in load_own:
        copy.start()
    load_values.start()
    load_layer = [
        pltpu.make_async_copy(weights_hbm, weights_ref, local_sem.at[3]),
        pltpu.make_async_copy(bias_hbm, bias_ref, local_sem.at[4]),
        pltpu.make_async_copy(cotangent_hbm, cotangent_ref, local_sem.at[5]),
    ]
    for copy in load_layer:
        copy.start()
    load_index = [
        pltpu.make_async_copy(rows_hbm, rows_ref, local_sem.at[6]),
        pltpu.make_async_copy(cols_hbm, cols_ref, local_sem.at[7]),
    ]
    for copy in load_index:
        copy.start()
    pl.semaphore_wait(barrier, len(peers))
    for copy in load_own:
        copy.wait()

    used = [0]
    bulk = [0, 0]
    staged = []

    def receive_slot():
        used[0] += 1
        return used[0] - 1

    def send(src, dst, to, slot=None, sent=None):
        if sent is None:
            sent = send_sem.at[bulk[0]]
            bulk[1] += math.prod(src.shape)
        copy = pltpu.make_async_remote_copy(
            src_ref=src,
            dst_ref=dst,
            send_sem=sent,
            recv_sem=recv_sem.at[receive_slot() if slot is None else slot],
            device_id=to,
            device_id_type=MESH,
        )
        copy.start()
        return copy

    def whole(ref, slot, sent):
        return pltpu.make_async_remote_copy(
            src_ref=ref,
            dst_ref=ref,
            send_sem=sent,
            recv_sem=recv_sem.at[slot],
            device_id=other_core,
            device_id_type=MESH,
        )

    def wait_group(ref, slot):
        whole(ref, slot, send_sem.at[0]).wait_recv()

    def drain():
        blocks = bulk[1] // (BS * BS)
        assert blocks * BS * BS == bulk[1] and blocks <= panel.shape[0]
        whole(panel.at[pl.ds(0, blocks)], 0, send_sem.at[bulk[0]]).wait_send()
        bulk[0] += 1
        bulk[1] = 0

    def share(piece, to, slot=None):
        return send(piece, piece, to, slot)

    def stage(copies, ref):
        slot = receive_slot()
        sent = stage_sem.at[len(staged)]
        for src, dst, to in copies:
            send(src, dst, to, slot, sent)
        staged.append(whole(ref, slot, sent))
        return staged[-1]

    up, down = device(at_z(1), x, y, k), device(at_z(-1), x, y, k)
    ways = ((1, up), (-1, down))
    x_steps = sorted(range(1, X), key=lambda d: -min(d, X - d))

    def shard(zz, xx, part):
        return panel.at[2 * (zz * X + xx) + part]

    halves = {1: pl.ds(0, BS // 2), -1: pl.ds(BS // 2, BS // 2)}
    final = receive_slot()

    a_x = {}
    for d in x_steps:
        a_x[d] = share(shard(z, x, 0), device(z, at_x(d), y, k))
    a_hop = {}
    b_hop = {}
    for s, to in ways:
        a_hop[s, 1, 0] = share(shard(z, x, 0), to)
        b_hop[s, 1] = share(shard(z, x, 1), to)
    for d in x_steps:
        share(shard(z, x, 1), device(z, at_x(d), y, k), final)
    values[slots] = jnp.zeros((BS, BS), BF16)
    fwd_groups = group_count(slots, slab_blocks, FWD_GROUP, FWD_UNROLL)
    bwd_groups = group_count(slots, col_blocks, BWD_GROUP, BWD_PARTS * BWD_UNROLL)
    for copy in load_index:
        copy.wait()
    live = iota((1, slots), 1) < live_ref[...]
    lists_vmem[0] = sorted_lists(
        rows_ref[0], cols_ref[0], live, slab_blocks, col_blocks, FWD_GROUP, fwd_groups
    )
    fetch_fwd = pltpu.make_async_copy(lists_vmem.at[0], fwd_list, local_sem.at[8])
    fetch_fwd.start()
    for d in reversed(x_steps):
        a_x[d].wait_recv()
        for s, to in ways:
            a_hop[s, 1, d] = share(shard(z, at_x(-d), 0), to)
    a_final = 0
    for h in range(1, half_z + 1):
        for s, to in ways:
            b_hop[s, h].wait_recv()
            piece = shard(at_z(-s * h), x, 1)
            if h + 1 < half_z:
                b_hop[s, h + 1] = share(piece, to)
            elif h + 1 == half_z:
                b_hop[s, h + 1] = share(piece.at[halves[s]], to)
            else:
                piece = piece.at[halves[s]]
            for d in x_steps:
                share(piece, device(z, at_x(d), y, k), final)
        for d in range(X):
            for s, to in ways:
                if h < half_z:
                    a_hop[s, h, d].wait_recv()
                    piece = shard(at_z(-s * h), at_x(-d), 0)
                    if h + 1 < half_z:
                        a_hop[s, h + 1, d] = share(piece, to)
                    elif (d < half_x) == (s > 0):
                        share(piece, to, final)
                        a_final += 1
    wait_group(panel.at[pl.ds(0, a_final + Z * (X - 1))], final)
    fetch_fwd.wait()
    load_values.wait()

    zero_block = jnp.zeros((BS, BS), F32)

    def run_groups(table, group, first, groups, unroll, left, right, total):
        def step(base, total):
            for u in range(unroll):
                t = first + base * unroll + u
                at = t * group
                lhs = [left(at + g) for g in range(group)]
                rhs = [right(at + g) for g in range(group)]
                product = jnp.dot(
                    jnp.concatenate(lhs, axis=1),
                    jnp.concatenate(rhs, axis=0),
                    preferred_element_type=F32,
                )
                total = product + total * table[2, t].astype(F32)
                sums[t] = total
            return total

        assert groups % unroll == 0
        return lax.fori_loop(0, groups // unroll, step, total)

    run_groups(
        fwd_list,
        FWD_GROUP,
        0,
        fwd_groups,
        FWD_UNROLL,
        lambda at: values[fwd_list[0, at]],
        lambda at: panel[fwd_list[1, at]],
        zero_block,
    )
    sums[fwd_groups] = zero_block

    drain()

    def row_pair(yy, kk, i):
        return sums[fwd_list[3, 2 * (yy * K + kk) + i]]

    y_steps = sorted(range(1, Y), key=lambda d: -min(d, Y - d))
    from_core = {}
    for d in y_steps + [0]:
        for i in range(2):
            core_out[d, i] = row_pair(at_y(d), 1 - k, i).astype(BF16)
        from_core[d] = send(core_out.at[d], core_in.at[d], other_core)
    from_y = {}
    for d in y_steps:
        from_core[d].wait_recv()
        for i in range(2):
            y_out[d, i] = (row_pair(at_y(d), k, i) + core_in[d, i].astype(F32)).astype(BF16)
            from_y[d, i] = send(y_out.at[d, i], y_in.at[d, i], device(z, x, at_y(d), k))
    lists_vmem[1] = sorted_lists(
        cols_ref[0], rows_ref[0], live, col_blocks, slab_blocks, BWD_GROUP, bwd_groups
    )
    fetch_bwd = pltpu.make_async_copy(lists_vmem.at[1], bwd_list, local_sem.at[9])
    fetch_bwd.start()
    from_core[0].wait_recv()
    own = [row_pair(y, k, i) + core_in[0, i].astype(F32) for i in range(2)]
    for d in y_steps:
        for i in range(2):
            from_y[d, i].wait_recv()
            own[i] = own[i] + y_in[d, i].astype(F32)
    aggregate = jnp.concatenate(own, axis=0).astype(BF16)

    for copy in load_layer:
        copy.wait()
    weights = weights_ref[...]
    preact = jnp.dot(aggregate, weights, preferred_element_type=F32) + bias_ref[...]
    sigma = 1.0 / (1.0 + jnp.exp(-preact))
    deriv = sigma * (1.0 + preact * (1.0 - sigma))
    grad_pre_wide = cotangent_ref[...].astype(F32) * deriv
    grad_pre = grad_pre_wide.astype(BF16)
    grad_t = lax.dot_general(
        weights, grad_pre, (((1,), (1,)), ((), ())), preferred_element_type=F32
    ).astype(BF16)
    agg_t[2 * c] = grad_t[:, 0:BS]
    agg_t[2 * c + 1] = grad_t[:, BS : 2 * BS]

    def slab_pair(yy, kk):
        return agg_t.at[pl.ds(2 * (yy * K + kk), 2)]

    from_y = {}
    for d in y_steps:
        from_y[d] = share(slab_pair(y, k), device(z, x, at_y(d), k))
    core_slot = receive_slot()
    share(slab_pair(y, k), other_core, core_slot)
    hidden_ref[...] = (preact * sigma).astype(BF16)
    weight_term = lax.dot_general(
        aggregate, grad_pre, (((0,), (0,)), ((), ())), preferred_element_type=F32
    )
    bias_term = jnp.sum(grad_pre.astype(F32), axis=0, keepdims=True)
    grad_weights_ref[...] = weight_term
    rows_core = BS // K
    rows_y = rows_core // Y
    w_tall = rows_y + 8
    rows_x = w_z.shape[1]

    def rows_at(start, size):
        return pl.ds(pl.multiple_of(start, 8), size)

    for i, kk in ((0, 1 - k), (1, k)):
        w_half[i, 0:rows_core] = grad_weights_ref[rows_at(kk * rows_core, rows_core), :]
        w_half[i, rows_core : rows_core + 8] = jnp.broadcast_to(bias_term, (8, bias_term.shape[1]))
    w_core = stage([(w_half.at[0], w_half_in, other_core)], w_half_in)
    for d in reversed(y_steps):
        from_y[d].wait_recv()
        share(slab_pair(at_y(-d), k), other_core, core_slot)
    w_core.wait_recv()
    w_half[1] = w_half[1] + w_half_in[...]
    bias_rows = w_half[1, rows_core : rows_core + 8]
    for d in range(Y):
        w_y[d, 0:rows_y] = w_half[1, rows_at(at_y(d) * rows_y, rows_y), :]
        w_y[d, rows_y:w_tall] = bias_rows
    w_from_y = stage(
        [(w_y.at[d], w_y_in.at[y], device(z, x, at_y(d), k)) for d in y_steps],
        w_y_in.at[pl.ds(0, Y - 1)],
    )
    w_y_in[y] = w_y[0]
    wait_group(agg_t.at[pl.ds(0, 2 * Y)], core_slot)

    w_copies = {}

    def stage_x():
        w_from_y.wait_recv()
        total = w_y_in[0]
        for yy in range(1, Y):
            total = total + w_y_in[yy]
        w_x[0:w_tall] = total
        if rows_x * X > w_tall:
            w_x[w_tall : rows_x * X] = jnp.zeros((rows_x * X - w_tall, total.shape[1]), F32)
        w_copies["x"] = stage(
            [
                (w_x.at[rows_at(at_x(d) * rows_x, rows_x)], w_x_in.at[x], device(z, at_x(d), y, k))
                for d in x_steps
            ],
            w_x_in.at[pl.ds(0, X - 1)],
        )
        w_x_in[x] = w_x[rows_at(x * rows_x, rows_x), :]

    def stage_z():
        w_copies["x"].wait_recv()
        total = w_x_in[0]
        for xx in range(1, X):
            total = total + w_x_in[xx]
        w_z[z] = total
        w_copies["z"] = stage(
            [(w_z.at[z], w_z.at[z], peer) for peer in z_peers], w_z.at[pl.ds(0, Z - 1)]
        )

    def stage_back_x():
        w_copies["z"].wait_recv()
        total = w_z[0]
        for zz in range(1, Z):
            total = total + w_z[zz]
        w_row[rows_at(x * rows_x, rows_x), :] = total
        mine = w_row.at[rows_at(x * rows_x, rows_x)]
        w_copies["bx"] = stage(
            [(mine, mine, device(z, at_x(d), y, k)) for d in x_steps],
            w_row.at[pl.ds(0, rows_x * (X - 1))],
        )

    def stage_back_y():
        w_copies["bx"].wait_recv()
        mine = rows_at(k * rows_core + y * rows_y, rows_y)
        w_full[mine, :] = w_row[0:rows_y]
        w_copies["by"] = stage(
            [(w_full.at[mine], w_full.at[mine], device(z, x, at_y(d), k)) for d in y_steps],
            w_full.at[pl.ds(0, rows_y * (Y - 1))],
        )

    def stage_back_core():
        w_copies["by"].wait_recv()
        mine = rows_at(k * rows_core, rows_core)
        w_copies["bc"] = stage([(w_full.at[mine], w_full.at[mine], other_core)], w_full.at[mine])

    stages = [stage_z, stage_back_x, stage_back_y, stage_back_core]

    fetch_bwd.wait()
    part_groups = bwd_groups // BWD_PARTS
    running = zero_block
    for part in range(BWD_PARTS):
        running = run_groups(
            bwd_list,
            BWD_GROUP,
            part * part_groups,
            part_groups,
            BWD_UNROLL,
            lambda at: agg_t[bwd_list[1, at]],
            lambda at: values[bwd_list[0, at]],
            running,
        )
        if part == 0:
            stage_x()
            drain()
    sums[bwd_groups] = zero_block

    def column(zz, xx, part):
        return sums[bwd_list[3, 2 * (zz * X + xx) + part]]

    a_hop = {}
    b_hop = {}
    b_x = {}
    x_slot = receive_slot()

    def send_a(s, to, h, d):
        if h == 1 and (d < half_x) != (s > 0):
            return
        i = 0 if s > 0 else 1
        total = column(at_z(s * (half_z - h + 1)), at_x(d), 0)
        if (s, h - 1, d) in a_hop:
            a_hop[s, h - 1, d].wait_recv()
            total = total + a_in[i, h - 2, d].astype(F32)
        a_out[i, h - 1, d] = total.astype(BF16)
        a_hop[s, h, d] = send(a_out.at[i, h - 1, d], a_in.at[i, h - 1, d], to)

    def send_bx(dz):
        b_x[dz % Z] = receive_slot()
        for i, d in enumerate(x_steps):
            bx_out[dz % Z, i] = column(at_z(dz), at_x(d), 1).astype(BF16)
            send(bx_out.at[dz % Z, i], bx_in.at[dz % Z, i], device(z, at_x(d), y, k), b_x[dz % Z])

    def sum_bx(dz):
        total = column(at_z(dz), x, 1)
        wait_group(bx_in.at[dz % Z, pl.ds(0, X - 1)], b_x[dz % Z])
        for i in range(X - 1):
            total = total + bx_in[dz % Z, i].astype(F32)
        return total

    def send_b(h):
        shared = sum_bx(half_z) if h == 1 else None
        for i, (s, to) in enumerate(ways):
            rows = slice(0, BS // 2) if s > 0 else slice(BS // 2, BS)
            if h == 1:
                b_out[i, 0, rows] = shared[rows].astype(BF16)
                b_hop[s, 1] = send(b_out.at[i, 0, halves[s]], b_in.at[i, 0, halves[s]], to)
                continue
            total = sum_bx(s * (half_z - h + 1))
            b_hop[s, h - 1].wait_recv()
            if h == 2:
                part = total[rows] + b_in[i, 0, rows].astype(F32)
                rest = total[BS // 2 : BS] if s > 0 else total[0 : BS // 2]
                total = jnp.concatenate([part, rest] if s > 0 else [rest, part], axis=0)
            else:
                total = total + b_in[i, h - 2].astype(F32)
            b_out[i, h - 1] = total.astype(BF16)
            b_hop[s, h] = send(b_out.at[i, h - 1], b_in.at[i, h - 1], to)

    for d in range(X):
        for s, to in ways:
            send_a(s, to, 1, d)
    send_bx(half_z)
    for h in range(half_z - 1, 1, -1):
        send_bx(h)
        send_bx(-h)
        if h == half_z - 1:
            stages.pop(0)()
    for h in range(2, half_z + 1):
        for d in range(X):
            for s, to in ways:
                send_a(s, to, h, d)
        send_b(h - 1)
        if stages:
            stages.pop(0)()
        if h == 2:
            for near in (1, -1, 0):
                send_bx(near)
    last_a = None
    for i, d in enumerate(x_steps + [0]):
        total = column(z, at_x(d), 0)
        for j, (s, _) in enumerate(ways):
            a_hop[s, half_z, d].wait_recv()
            total = total + a_in[j, half_z - 1, d].astype(F32)
        if d:
            ax_out[i] = total.astype(BF16)
            send(ax_out.at[i], ax_in.at[i], device(z, at_x(d), y, k), x_slot)
        else:
            last_a = total
    send_b(half_z)
    while stages:
        stages.pop(0)()
    last_b = sum_bx(0)
    wait_group(ax_in.at[pl.ds(0, X - 1)], x_slot)
    for i in range(X - 1):
        last_a = last_a + ax_in[i].astype(F32)
    grad_features_ref[0:BS, :] = last_a.T
    grad_bias_ref[...] = w_row[rows_y : rows_y + 1] * scale
    w_copies["bc"].wait_recv()
    grad_weights_ref[...] = w_full[...] * scale
    drain()
    for i, (s, _) in enumerate(ways):
        b_hop[s, half_z].wait_recv()
        last_b = last_b + b_in[i, half_z - 1].astype(F32)
    grad_features_ref[BS : 2 * BS, :] = last_b.T
    for copy in staged:
        copy.wait_send()


def mesh_dims(mesh):
    rows, rep = mesh.shape["rows"], mesh.shape["rep"]
    across = 4 if rows >= 32 else 2
    return rows // across, across, rep // 2, 2


def shards(
    dims, features, weights, bias_vector, block_values, block_rows, block_cols, block_live, cotangent
):
    Z, X, Y, K = dims
    nodes, width = features.shape
    hid = weights.shape[1]
    slots = block_values.shape[2]
    half_z = Z // 2
    groups = max(
        group_count(slots, 2 * Y * K, FWD_GROUP, FWD_UNROLL),
        group_count(slots, 2 * Z * X, BWD_GROUP, BWD_PARTS * BWD_UNROLL),
    )
    rows_y = BS // K // Y
    rows_x = -(-(rows_y + 8) // (8 * X)) * 8
    scale = 1.0 / math.sqrt(nodes * Z * X * Y * K)
    vmem = pl.BlockSpec(memory_space=pltpu.VMEM)
    hbm = pl.BlockSpec(memory_space=pltpu.HBM)
    block = (BS, BS)
    out = pl.pallas_call(
        functools.partial(kernel, dims, scale),
        out_shape=(
            pltpu.VMEM((nodes, hid), BF16),
            pltpu.VMEM((nodes, width), F32),
            pltpu.VMEM((width, hid), F32),
            pltpu.VMEM((1, hid), F32),
        ),
        in_specs=[
            hbm,
            hbm,
            hbm,
            hbm,
            hbm,
            hbm,
            vmem,
            hbm,
        ],
        out_specs=(vmem, vmem, vmem, vmem),
        scratch_shapes=[
            pltpu.SMEM((8, LIST_WIDTH), jnp.int32),
            pltpu.SMEM((8, LIST_WIDTH), jnp.int32),
            pltpu.VMEM((2, 8, LIST_WIDTH), jnp.int32),
            pltpu.VMEM(block_rows.shape, jnp.int32),
            pltpu.VMEM(block_cols.shape, jnp.int32),
            pltpu.VMEM((slots + 1, *block), BF16),
            pltpu.VMEM((width, hid), BF16),
            pltpu.VMEM((1, hid), F32),
            pltpu.VMEM((nodes, hid), BF16),
            pltpu.VMEM((2 * Z * X, *block), BF16),
            pltpu.VMEM((groups + 1, *block), F32),
            pltpu.VMEM((Y, 2, *block), BF16),
            pltpu.VMEM((Y, 2, *block), BF16),
            pltpu.VMEM((Y, 2, *block), BF16),
            pltpu.VMEM((Y, 2, *block), BF16),
            pltpu.VMEM((2 * Y * K, *block), BF16),
            pltpu.VMEM((2, half_z, X, *block), BF16),
            pltpu.VMEM((2, half_z, X, *block), BF16),
            pltpu.VMEM((X, *block), BF16),
            pltpu.VMEM((X, *block), BF16),
            pltpu.VMEM((Z, X, *block), BF16),
            pltpu.VMEM((Z, X, *block), BF16),
            pltpu.VMEM((2, half_z, *block), BF16),
            pltpu.VMEM((2, half_z, *block), BF16),
            pltpu.VMEM((2, BS // K + 8, hid), F32),
            pltpu.VMEM((BS // K + 8, hid), F32),
            pltpu.VMEM((Y, rows_y + 8, hid), F32),
            pltpu.VMEM((Y, rows_y + 8, hid), F32),
            pltpu.VMEM((rows_x * X, hid), F32),
            pltpu.VMEM((X, rows_x, hid), F32),
            pltpu.VMEM((Z, rows_x, hid), F32),
            pltpu.VMEM((rows_x * X, hid), F32),
            pltpu.VMEM((BS, hid), F32),
            pltpu.SemaphoreType.DMA((SEND_SLOTS,)),
            pltpu.SemaphoreType.DMA((RECV_SLOTS,)),
            pltpu.SemaphoreType.DMA((STAGES,)),
            pltpu.SemaphoreType.DMA((10,)),
        ],
        compiler_params=pltpu.CompilerParams(
            collective_id=0, has_side_effects=True, vmem_limit_bytes=63 * 1024 * 1024
        ),
        name="layer",
    )(
        features,
        weights,
        bias_vector.reshape(1, hid),
        block_values,
        block_rows,
        block_cols,
        block_live,
        cotangent,
    )
    hidden, grad_features, grad_weights, grad_bias = out
    return hidden, grad_features, grad_weights, grad_bias.reshape(hid)


def solution(mesh):
    in_specs = (
        P(("rows", "rep"), None),
        P(),
        P(),
        P("rows", "rep", None, None, None),
        P("rows", "rep", None),
        P("rows", "rep", None),
        P("rows", "rep"),
        P(("rows", "rep"), None),
    )
    out_specs = (P(("rows", "rep"), None), P(("rows", "rep"), None), P(), P())
    return jax.shard_map(
        functools.partial(shards, mesh_dims(mesh)),
        mesh=mesh,
        in_specs=in_specs,
        out_specs=out_specs,
        check_vma=False,
    )
```
